128 devices in a mesh: inline: 16 (over x, z), xline: 8 (over y, core).
Axes of the slice: x: 4, y: 4, z: 4, core: 2. Of those that a mesh axis runs over, the one named last changes fastest.
Arguments:
- traces: bfloat16 [32768, 2048], P(('inline', 'xline')), may hold values from -6 to 6
- trace_dest: int32 [32768, 1], P(('inline', 'xline')), may hold values from 0 to 127; in each aligned block of 256 rows (0 to 255, 256 to 511, ...) at most 4 rows name the same one
- trace_bin: int32 [32768], P(('inline', 'xline')), may hold values from 0 to 3
- trace_class: int32 [32768], P(('inline', 'xline')), may hold values from 0 to 7
- band_weights: bfloat16 [8, 16, 2, 128, 128], replicated, may hold values from -0.375 to 0.375
- conv_first: bfloat16 [32, 8, 3, 3, 3], replicated, may hold values from -0.4375 to 0.4375
- conv_second: bfloat16 [32, 32, 3, 3, 3], replicated, may hold values from -0.21875 to 0.21875
Outputs:
- regular: bfloat16 [32, 32, 16, 2048], P(None, 'inline', 'xline')
The draws below stay inside these ranges and needn't reach their ends.
Inputs may be any that keep to these rules, and one draw needn't show every extreme that they name: `trace_dest`: among the 256 traces of one device no tile is named more than 4 times, a bound that some block reaches.
All inputs are finite; a program needn't handle non-finite values.
Results may differ from the reference program's by a relative error of at most 0.0065.
Values may be sent and summed in bfloat16 or wider, within the bound.
No kernel may reach another device: no remote copies, remote signals or barrier semaphores. Data moves between devices by JAX's collectives and lax.ppermute only.
A program may use at most 256 MiB of HBM per device.

```python
import math
import jax
import jax.numpy as jnp
import numpy as np
from jax import lax

NS = 2048
CH = 32
CLASSES = 8
BAND = 128
BI = 2
BX = 2
TR_DEV = 256
CAP = 4
NB = 16
TRACES = 32768
INLINE_BINS = 32
XLINE_BINS = 16
N_XLINE = 8
DEVICES = 128


def place_ends(array, rng, least, high):
    index_at = [jax.random.randint(jax.random.fold_in(rng, axis), (), 0, length) for axis, length in enumerate(array.shape)]
    widest = array.shape.index(max(array.shape))
    neighbour = index_at[:widest] + [(index_at[widest] + 1) % array.shape[widest]] + index_at[widest + 1:]
    return array.at[tuple(index_at)].set(least).at[tuple(neighbour)].set(high)


def shard_levels(own_key, dims, cuts, smallest, largest):
    gain = 1.0
    for position, parts in cuts:
        steps = jax.random.uniform(jax.random.fold_in(jax.random.fold_in(own_key, 6), position), (parts,), jnp.float32, smallest / len(cuts), largest / len(cuts))
        gain = gain * jnp.repeat(jnp.exp(steps), dims[position] // parts).reshape((-1,) + (1,) * (len(dims) - 1 - position))
    return gain


def assign_block(key, own, number, rows, count, top, most, lean):
    order = jax.random.permutation(key, count)
    crowded, ordinary = shares(count, rows * top, most, lean, True), shares(count, rows * top, most, lean, False)
    places = jnp.arange(count)

    def named(tallies, offset_by):
        used = int((tallies > 0).sum())
        fixed = max(1, used // 4)
        passed = fixed + (places - fixed + offset_by * (used - fixed)) % max(1, count - fixed)
        return jnp.zeros((count,), jnp.int32).at[order[jnp.where(places < fixed, places, passed)]].set(jnp.asarray(tallies, jnp.int32))

    tallies = jnp.where(number % 4 == 0, named(crowded, number // 4), named(ordinary, number - number // 4 - 1))
    mixed = jax.random.permutation(jax.random.fold_in(own, 3), count)
    source_of, receiver = mixed[0:count // 2 * 2:2], mixed[1:count // 2 * 2:2]
    slack = jnp.minimum(tallies[source_of] - 1, most - tallies[receiver]) // 2
    slack = jnp.where((source_of == order[0]) | (receiver == order[0]) | (tallies[receiver] == 0), 0, jnp.maximum(slack, 0))
    passed = jax.random.randint(jax.random.fold_in(own, 4), (count // 2,), 0, 1 << 20) % (slack + 1)
    tallies = tallies.at[source_of].add(-passed).at[receiver].add(passed)
    members = jnp.searchsorted(jnp.cumsum(tallies), jnp.arange(rows * top), side="right").astype(jnp.int32)
    table = members.reshape(top, rows).T
    table = table[jax.random.permutation(jax.random.fold_in(own, 1), rows)]
    offset_by = jax.random.randint(jax.random.fold_in(own, 2), (rows, 1), 0, top)
    return jnp.take_along_axis(table, (jnp.arange(top)[None, :] + offset_by) % top, axis=1)


def shares(amount, total, bound, skew, full):
    loads = [(1 << 20) // math.isqrt(standing ** skew) + 1 for standing in range(1, amount + 1)]
    largest = bound if full else min(bound, max(-(-total // amount), total * loads[0] // sum(loads)))
    least = 1 if total - largest >= amount - 1 else 0
    holding, surplus = [largest] + [least] * (amount - 1), total - largest - least * (amount - 1)
    while surplus > 0:
        candidates = [i for i in range(1, amount) if holding[i] < largest] or [i for i in range(1, amount) if holding[i] < bound]
        mass, remaining = sum([loads[i] for i in candidates]), surplus
        for i in candidates:
            extra = min(bound - holding[i], max(1, remaining * loads[i] // mass), surplus)
            holding[i] = holding[i] + extra
            surplus = surplus - extra
    return np.array(holding)


def noise(stream_key, shape, deviation, limit, cuts=(), dtype=jnp.bfloat16):
    gain = shard_levels(stream_key, shape, cuts, -0.22, 0.18) if cuts else 1.0
    drawn = jax.random.normal(stream_key, shape, jnp.float32) * deviation * gain
    return jnp.minimum(jnp.maximum(drawn, -limit), limit).astype(dtype)


def setup_inputs(seed: int = 0) -> dict:
    key_list = jax.random.split(jax.random.key(seed), 8)
    traces = noise(key_list[0], (TRACES, NS), 1.0, 6.0, ((0, 128),))
    trace_dest_keys = jax.random.split(jax.random.fold_in(key_list[1], 1), TRACES // TR_DEV)
    trace_dest_turns = jax.random.permutation(jax.random.fold_in(key_list[1], 3), TRACES // TR_DEV)
    trace_dest = jax.vmap(lambda own, number: assign_block(jax.random.fold_in(key_list[1], 2), own, number, TR_DEV, DEVICES, 1, CAP, 2))(trace_dest_keys, trace_dest_turns).reshape((TRACES, 1))
    trace_bin = place_ends(jax.random.randint(key_list[2], (TRACES,), 0, BI * BX), jax.random.fold_in(key_list[2], 1), 0, (BI * BX) - 1).astype(jnp.int32)
    trace_class = place_ends(jax.random.randint(key_list[3], (TRACES,), 0, CLASSES), jax.random.fold_in(key_list[3], 1), 0, CLASSES - 1).astype(jnp.int32)
    band_weights = noise(key_list[4], (CLASSES, NB, 2, BAND, BAND), (2 * BAND) ** -0.5, 0.375)
    conv_first = noise(key_list[5], (CH, CLASSES, 3, 3, 3), (27 * CLASSES) ** -0.5, 0.4375)
    conv_second = noise(key_list[6], (CH, CH, 3, 3, 3), (27 * CH) ** -0.5, 0.21875)
    return {"traces": traces, "trace_dest": trace_dest, "trace_bin": trace_bin, "trace_class": trace_class, "band_weights": band_weights, "conv_first": conv_first, "conv_second": conv_second}


def convolve(volume, kernel):
    return lax.conv_general_dilated(volume[None].astype(jnp.float32), kernel.astype(jnp.float32), (1, 1, 1), "SAME", dimension_numbers=("NCDHW", "OIDHW", "NCDHW"))[0]


def reference(traces, trace_dest, trace_bin, trace_class, band_weights, conv_first, conv_second):
    target = trace_dest[:, 0]
    inline_bin = (target // N_XLINE) * BI + trace_bin // BX
    xline_bin = (target % N_XLINE) * BX + trace_bin % BX
    segment = ((trace_class * INLINE_BINS + inline_bin) * XLINE_BINS + xline_bin).astype(jnp.int32)
    total = CLASSES * INLINE_BINS * XLINE_BINS
    stacked = jax.ops.segment_sum(traces.astype(jnp.float32), segment, num_segments=total)
    fold_count = jax.ops.segment_sum(jnp.ones(segment.shape, jnp.float32), segment, num_segments=total)
    averaged = (stacked / jnp.maximum(fold_count, 1.0)[:, None]).astype(jnp.bfloat16)
    blocks = averaged.reshape(CLASSES, INLINE_BINS * XLINE_BINS, NB, BAND).astype(jnp.float32)
    following = jnp.concatenate([blocks[:, :, 1:], jnp.zeros_like(blocks[:, :, :1])], axis=2)
    band_f = band_weights.astype(jnp.float32)
    shifted = jnp.einsum("cbkt,cktu->cbku", blocks, band_f[:, :, 0]) + jnp.einsum("cbkt,cktu->cbku", following, band_f[:, :, 1])
    volume = shifted.astype(jnp.bfloat16).reshape(CLASSES, INLINE_BINS, XLINE_BINS, NS)
    hidden = jax.nn.gelu(convolve(volume, conv_first)).astype(jnp.bfloat16)
    return convolve(hidden, conv_second).astype(jnp.bfloat16)
```

```python
import jax
import jax.numpy as jnp
import numpy as np
from jax import lax
from jax.experimental import pallas as pl
from jax.experimental.pallas import tpu as pltpu
from jax.sharding import PartitionSpec as P

CLASSES = 8
BI = 2
BX = 2
CH = 32
CAP = 4
ALL = ("inline", "xline")
BF = jnp.bfloat16
F32 = jnp.float32
CELLS = CLASSES * BI * BX


def iota(shape, dim):
    return lax.broadcasted_iota(jnp.int32, shape, dim)


def nt(a, b):
    return lax.dot_general(a, b, (((1,), (1,)), ((), ())), preferred_element_type=F32)


def tn(a, b):
    return lax.dot_general(a, b, (((0,), (0,)), ((), ())), preferred_element_type=F32)


def nn(a, b):
    return jnp.dot(a, b, preferred_element_type=F32)


def before(count):
    return (iota((count, count), 0) < iota((count, count), 1)).astype(BF)


def pack_kernel(dest_ref, bin_ref, class_ref, traces_ref, out_ref, tags, loaded, packed, tag_sem, load_sem, store_sem):
    rows, width = packed.shape
    count, half = loaded.shape[0] // 2, loaded.shape[1]
    devices = rows // (2 * CAP)
    strips = load_sem.shape[0]
    tile = half // strips
    small = []
    for number, ref in enumerate((dest_ref, bin_ref, class_ref)):
        small.append(pltpu.make_async_copy(ref, tags.at[number], tag_sem.at[number]))
        small[-1].start()
    loads = []
    for strip in range(strips):
        for side in range(2):
            loads.append(
                pltpu.make_async_copy(
                    traces_ref.at[:, pl.ds(side * half + strip * tile, tile)],
                    loaded.at[pl.ds(side * count, count), pl.ds(strip * tile, tile)],
                    load_sem.at[strip, side],
                )
            )
            loads[-1].start()
    for copy in small:
        copy.wait()
    dest = tags[0]
    named = iota((devices, count), 0) == dest
    rank = nn(named.astype(BF), before(count))
    slot = jnp.sum(jnp.where(named, rank, 0.0), axis=0, keepdims=True)
    position = dest * (2 * CAP) + slot.astype(jnp.int32)
    row = iota((rows, count), 0)
    place = jnp.concatenate(
        [(row == position).astype(BF), (row == position + CAP).astype(BF)], axis=1
    )
    cell = tags[1] * CLASSES + tags[2]
    lane = iota((128, count), 0)
    tagged = jnp.concatenate(
        [((lane == cell) | (lane == 127)).astype(BF), (lane == cell + CELLS).astype(BF)], axis=1
    )
    stores = []

    def store(at, size, number):
        copy = pltpu.make_async_copy(
            packed.at[:, pl.ds(at, size)], out_ref.at[:, pl.ds(at, size)], store_sem.at[number]
        )
        copy.start()
        stores.append(copy)

    packed[:, half:] = nt(place, tagged).astype(BF)
    store(half, 128, strips)
    for strip in range(strips):
        loads[2 * strip].wait()
        loads[2 * strip + 1].wait()
        at = strip * tile
        packed[:, at : at + tile] = nn(place, loaded[:, at : at + tile]).astype(BF)
        store(at, tile, strip)
    for copy in stores:
        copy.wait()


def pack(traces, dest, bins, classes, devices):
    count, samples = traces.shape
    rows, width = devices * 2 * CAP, samples // 2 + 128
    strips = 4
    kept = pl.BlockSpec(memory_space=pltpu.HBM)
    pin = lambda array: pltpu.with_memory_space_constraint(array, pltpu.HBM)
    return pl.pallas_call(
        pack_kernel,
        in_specs=[kept] * 4,
        out_specs=kept,
        out_shape=pltpu.HBM((rows, width), BF),
        scratch_shapes=[
            pltpu.VMEM((3, 1, count), jnp.int32),
            pltpu.VMEM((2 * count, samples // 2), BF),
            pltpu.VMEM((rows, width), BF),
            pltpu.SemaphoreType.DMA((3,)),
            pltpu.SemaphoreType.DMA((strips, 2)),
            pltpu.SemaphoreType.DMA((strips + 1,)),
        ],
        compiler_params=pltpu.CompilerParams(vmem_limit_bytes=40 << 20),
        name="pack",
    )(pin(dest), pin(bins), pin(classes), pin(traces))


def stack_kernel(arrived_ref, band_ref, out_ref, averaged, weights, sem):
    width = arrived_ref.shape[1]
    half = width - 128
    parts, _, each, _, band = weights.shape
    loads = []
    for part in range(parts):
        loads.append(
            pltpu.make_async_copy(
                band_ref.at[:, pl.ds(part * each, each)], weights.at[part], sem.at[part]
            )
        )
        loads[-1].start()
    stacked = tn(arrived_ref[:, half:], arrived_ref[...])
    fold = jnp.maximum(stacked[:CELLS, width - 1 : width], 1.0)
    averaged[:, :half] = (stacked[:CELLS, :half] / fold).astype(BF)
    averaged[:, half : 2 * half] = (stacked[CELLS : 2 * CELLS, :half] / fold).astype(BF)
    averaged[:, 2 * half :] = jnp.zeros((CELLS, band), BF)
    kind = iota((CELLS, band), 0) % CLASSES
    for block in range(parts * each):
        if block % each == 0:
            loads[block // each].wait()
        start = block * band
        pair = averaged[:, start : start + 2 * band]
        wide = jnp.concatenate(
            [weights[block // each, number, block % each] for number in range(CLASSES)], axis=1
        )
        moved = nn(pair, wide)
        total = moved[:, :band]
        for number in range(1, CLASSES):
            total = jnp.where(kind == number, moved[:, number * band : (number + 1) * band], total)
        out_ref[:, start : start + band] = total.astype(BF)


def stack(arrived, band_weights):
    rows, width = arrived.shape
    samples = 2 * (width - 128)
    classes, blocks, steps, band, _ = band_weights.shape
    weights = band_weights.reshape(classes, blocks, steps * band, band)
    parts = 8
    whole = pl.BlockSpec(memory_space=pltpu.VMEM)
    return pl.pallas_call(
        stack_kernel,
        in_specs=[whole, pl.BlockSpec(memory_space=pltpu.HBM)],
        out_specs=whole,
        out_shape=jax.ShapeDtypeStruct((CELLS, samples), BF),
        scratch_shapes=[
            pltpu.VMEM((CELLS, samples + band), BF),
            pltpu.VMEM((parts, classes, blocks // parts, steps * band, band), BF),
            pltpu.SemaphoreType.DMA((parts,)),
        ],
        compiler_params=pltpu.CompilerParams(vmem_limit_bytes=24 << 20),
        name="stack",
    )(arrived, pltpu.with_memory_space_constraint(weights, pltpu.HBM))


def later(value):
    rolled = pltpu.roll(value, 1, 1)
    return jnp.where(iota(value.shape, 1) == 0, 0.0, rolled)


def sooner(value):
    samples = value.shape[1]
    rolled = pltpu.roll(value, samples - 1, 1)
    return jnp.where(iota(value.shape, 1) == samples - 1, 0.0, rolled)


def conv_kernel(place_ref, mid_ref, low_ref, high_ref, first_ref, second_ref, out_ref, taps, hidden):
    samples = mid_ref.shape[1]
    tall = BX * CLASSES
    group = 9 * tall
    for which, ref in enumerate((low_ref, mid_ref, high_ref)):
        value = ref[...].astype(F32)
        for tap, shifted in enumerate((later(value), value, sooner(value))):
            shifted = shifted.astype(BF)
            for line in range(BI + 4):
                at = line * group + (tap * 3 + which) * tall
                taps[at : at + tall, :] = shifted[line * tall : (line + 1) * tall]
    wide = (BX + 2) * CH
    bin_x = iota((wide, 1), 0) // CH + place_ref[1] * BX - 1
    inside_x = (bin_x >= 0) & (bin_x < place_ref[3])
    first = first_ref[...]
    tile = 512
    for line in range(BI + 2):
        bin_i = line + place_ref[0] * BI - 1
        inside = inside_x & (bin_i >= 0) & (bin_i < place_ref[2])
        for start in range(0, samples, tile):
            window = taps[line * group : (line + 3) * group, start : start + tile]
            value = jax.nn.gelu(nn(first, window))
            value = jnp.where(inside, value, 0.0)
            hidden[line * wide : (line + 1) * wide, start : start + tile] = value.astype(BF)
    second = second_ref[...]
    value = nn(second, hidden[...])
    rows = CH * BI * BX
    total = value[rows : 2 * rows] + later(value[:rows]) + sooner(value[2 * rows :])
    out_ref[...] = total.astype(BF).reshape(out_ref.shape)


def convolutions(place, mid, low, high, first, second):
    samples = mid.shape[1]
    whole = pl.BlockSpec(memory_space=pltpu.VMEM)
    return pl.pallas_call(
        conv_kernel,
        in_specs=[pl.BlockSpec(memory_space=pltpu.SMEM)] + [whole] * 5,
        out_specs=whole,
        out_shape=jax.ShapeDtypeStruct((CH, BI, BX, samples), BF),
        scratch_shapes=[
            pltpu.VMEM(((BI + 4) * 9 * BX * CLASSES, samples), BF),
            pltpu.VMEM(((BI + 2) * (BX + 2) * CH, samples), BF),
        ],
        compiler_params=pltpu.CompilerParams(vmem_limit_bytes=48 << 20),
        name="convolutions",
    )(place, mid, low, high, first, second)


def first_matrix(kernel):
    spatial = kernel.transpose(2, 3, 4, 1, 0)
    placed = [
        jnp.pad(spatial, ((0, 0), (at, BX + 1 - at), (0, 0), (0, 0), (0, 0))) for at in range(BX + 2)
    ]
    matrix = jnp.stack(placed, axis=0)
    matrix = matrix.transpose(0, 5, 1, 3, 2, 4)
    return matrix.reshape((BX + 2) * CH, 9 * (BX + 4) * CLASSES)


def second_matrix(kernel):
    spatial = kernel.transpose(2, 3, 4, 0, 1)
    placed = [
        [
            jnp.pad(spatial, ((i, BI - 1 - i), (x, BX - 1 - x), (0, 0), (0, 0), (0, 0)))
            for x in range(BX)
        ]
        for i in range(BI)
    ]
    matrix = jnp.stack([jnp.stack(line, axis=0) for line in placed], axis=0)
    matrix = matrix.transpose(4, 5, 0, 1, 2, 3, 6)
    return matrix.reshape(3 * CH * BI * BX, (BI + 2) * (BX + 2) * CH)


def neighbours(block, axis):
    count = lax.axis_size(axis)
    forward = [(i, i + 1) for i in range(count - 1)]
    backward = [(target, source) for source, target in forward]
    return lax.ppermute(block, axis, forward), lax.ppermute(block, axis, backward)


def per_device(traces, trace_dest, trace_bin, trace_class, band_weights, conv_first, conv_second):
    inline_size = lax.axis_size("inline")
    xline_size = lax.axis_size("xline")
    devices = inline_size * xline_size
    at_i, at_x = lax.axis_index("inline"), lax.axis_index("xline")
    count, samples = traces.shape
    width = samples // 2 + 128
    outgoing = pack(
        traces,
        trace_dest.reshape(1, count),
        trace_bin.reshape(1, count),
        trace_class.reshape(1, count),
        devices,
    )
    arrived = lax.all_to_all(
        outgoing.reshape(devices, 2 * CAP, width), ALL, split_axis=0, concat_axis=0, tiled=True
    ).reshape(devices * 2 * CAP, width)
    first, second = first_matrix(conv_first), second_matrix(conv_second)
    arrived, first, second = lax.optimization_barrier((arrived, first, second))
    volume = stack(arrived, band_weights)
    before_i, after_i = neighbours(volume, "inline")
    column = jnp.concatenate([before_i, volume, after_i], axis=0)
    before_x, after_x = neighbours(column, "xline")
    place = jnp.stack(
        [at_i, at_x, jnp.int32(inline_size * BI), jnp.int32(xline_size * BX)]
    ).astype(jnp.int32)
    return convolutions(place, column, before_x, after_x, first, second)


def solution(mesh):
    return jax.shard_map(
        per_device,
        mesh=mesh,
        in_specs=(
            P(ALL, None),
            P(ALL, None),
            P(ALL),
            P(ALL),
            P(),
            P(),
            P(),
        ),
        out_specs=P(None, "inline", "xline", None),
        check_vma=False,
    )
```

```python
import jax
import jax.numpy as jnp
import numpy as np
from jax import lax
from jax.experimental import pallas as pl
from jax.experimental.pallas import tpu as pltpu
from jax.sharding import PartitionSpec as P

CLASSES = 8
BI = 2
BX = 2
CH = 32
CAP = 4
ALL = ("inline", "xline")
BF = jnp.bfloat16
F32 = jnp.float32
CELLS = CLASSES * BI * BX


def iota(shape, dim):
    return lax.broadcasted_iota(jnp.int32, shape, dim)


def nt(a, b):
    return lax.dot_general(a, b, (((1,), (1,)), ((), ())), preferred_element_type=F32)


def tn(a, b):
    return lax.dot_general(a, b, (((0,), (0,)), ((), ())), preferred_element_type=F32)


def nn(a, b):
    return jnp.dot(a, b, preferred_element_type=F32)


def before(count):
    return (iota((count, count), 0) < iota((count, count), 1)).astype(BF)


def pack_kernel(
    dest_ref, bin_ref, class_ref, traces_ref, out_ref, tags, loaded, packed, tag_sem, load_sem, store_sem
):
    rows, width = packed.shape
    count, half = loaded.shape[0] // 2, loaded.shape[1]
    devices = rows // (2 * CAP)
    parts = store_sem.shape[0]
    each = rows // parts
    small = []
    for number, ref in enumerate((dest_ref, bin_ref, class_ref)):
        small.append(pltpu.make_async_copy(ref, tags.at[number], tag_sem.at[number]))
        small[-1].start()
    loads = []
    for side in range(2):
        loads.append(
            pltpu.make_async_copy(
                traces_ref.at[:, pl.ds(side * half, half)],
                loaded.at[pl.ds(side * count, count)],
                load_sem.at[side],
            )
        )
        loads[-1].start()
    for copy in small:
        copy.wait()
    dest = tags[0]
    named = iota((devices, count), 0) == dest
    rank = nn(named.astype(BF), before(count))
    slot = jnp.sum(jnp.where(named, rank, 0.0), axis=0, keepdims=True)
    position = dest * (2 * CAP) + slot.astype(jnp.int32)
    row = iota((rows, count), 0)
    place = jnp.concatenate(
        [(row == position).astype(BF), (row == position + CAP).astype(BF)], axis=1
    )
    cell = tags[1] * CLASSES + tags[2]
    lane = iota((128, count), 0)
    tagged = jnp.concatenate(
        [((lane == cell) | (lane == 127)).astype(BF), (lane == cell + CELLS).astype(BF)], axis=1
    )
    for load in loads:
        load.wait()
    stores = []
    for part in range(parts):
        piece = slice(part * each, (part + 1) * each)
        packed[piece, half:] = nt(place[piece], tagged).astype(BF)
        packed[piece, :half] = nn(place[piece], loaded[...]).astype(BF)
        chunk = pl.ds(part * each, each)
        stores.append(pltpu.make_async_copy(packed.at[chunk], out_ref.at[chunk], store_sem.at[part]))
        stores[-1].start()
    for copy in stores:
        copy.wait()


def pack(traces, dest, bins, classes, devices):
    count, samples = traces.shape
    rows, width = devices * 2 * CAP, samples // 2 + 128
    kept = pl.BlockSpec(memory_space=pltpu.HBM)
    pin = lambda array: pltpu.with_memory_space_constraint(array, pltpu.HBM)
    return pl.pallas_call(
        pack_kernel,
        in_specs=[kept] * 4,
        out_specs=kept,
        out_shape=pltpu.HBM((rows, width), BF),
        scratch_shapes=[
            pltpu.VMEM((3, 1, count), jnp.int32),
            pltpu.VMEM((2 * count, samples // 2), BF),
            pltpu.VMEM((rows, width), BF),
            pltpu.SemaphoreType.DMA((3,)),
            pltpu.SemaphoreType.DMA((2,)),
            pltpu.SemaphoreType.DMA((4,)),
        ],
        compiler_params=pltpu.CompilerParams(vmem_limit_bytes=24 << 20),
        name="pack",
    )(pin(dest), pin(bins), pin(classes), pin(traces))


def stack_kernel(arrived_ref, band_ref, out_ref, averaged, weights, sem):
    width = arrived_ref.shape[1]
    half = width - 128
    parts, _, each, _, band = weights.shape
    loads = []
    for part in range(parts):
        loads.append(
            pltpu.make_async_copy(
                band_ref.at[:, pl.ds(part * each, each)], weights.at[part], sem.at[part]
            )
        )
        loads[-1].start()
    stacked = tn(arrived_ref[:, half:], arrived_ref[...])
    fold = jnp.maximum(stacked[:CELLS, width - 1 : width], 1.0)
    averaged[:, :half] = (stacked[:CELLS, :half] / fold).astype(BF)
    averaged[:, half : 2 * half] = (stacked[CELLS : 2 * CELLS, :half] / fold).astype(BF)
    averaged[:, 2 * half :] = jnp.zeros((CELLS, band), BF)
    kind = iota((CELLS, band), 0) % CLASSES
    for block in range(parts * each):
        if block % each == 0:
            loads[block // each].wait()
        start = block * band
        pair = averaged[:, start : start + 2 * band]
        wide = jnp.concatenate(
            [weights[block // each, number, block % each] for number in range(CLASSES)], axis=1
        )
        moved = nn(pair, wide)
        total = moved[:, :band]
        for number in range(1, CLASSES):
            total = jnp.where(kind == number, moved[:, number * band : (number + 1) * band], total)
        out_ref[:, start : start + band] = total.astype(BF)


def stack(arrived, band_weights):
    rows, width = arrived.shape
    samples = 2 * (width - 128)
    classes, blocks, steps, band, _ = band_weights.shape
    weights = band_weights.reshape(classes, blocks, steps * band, band)
    parts = 8
    whole = pl.BlockSpec(memory_space=pltpu.VMEM)
    return pl.pallas_call(
        stack_kernel,
        in_specs=[whole, pl.BlockSpec(memory_space=pltpu.HBM)],
        out_specs=whole,
        out_shape=jax.ShapeDtypeStruct((CELLS, samples), BF),
        scratch_shapes=[
            pltpu.VMEM((CELLS, samples + band), BF),
            pltpu.VMEM((parts, classes, blocks // parts, steps * band, band), BF),
            pltpu.SemaphoreType.DMA((parts,)),
        ],
        compiler_params=pltpu.CompilerParams(vmem_limit_bytes=24 << 20),
        name="stack",
    )(arrived, pltpu.with_memory_space_constraint(weights, pltpu.HBM))


def later(value):
    rolled = pltpu.roll(value, 1, 1)
    return jnp.where(iota(value.shape, 1) == 0, 0.0, rolled)


def sooner(value):
    samples = value.shape[1]
    rolled = pltpu.roll(value, samples - 1, 1)
    return jnp.where(iota(value.shape, 1) == samples - 1, 0.0, rolled)


def fill(taps, refs):
    tall = BX * CLASSES
    group = 3 * len(refs) * tall
    for which, ref in enumerate(refs):
        value = ref[...].astype(F32)
        for tap, shifted in enumerate((later(value), value, sooner(value))):
            shifted = shifted.astype(BF)
            for line in range(BI + 4):
                at = line * group + (tap * len(refs) + which) * tall
                taps[at : at + tall, :] = shifted[line * tall : (line + 1) * tall]
    return group


def inside(place_ref, start_x, line):
    bin_x = iota((BX * CH, 1), 0) // CH + start_x + place_ref[1] * BX - 1
    bin_i = line + place_ref[0] * BI - 1
    return (bin_x >= 0) & (bin_x < place_ref[3]) & (bin_i >= 0) & (bin_i < place_ref[2])


def joined(value):
    rows = value.shape[0] // 3
    return value[rows : 2 * rows] + later(value[:rows]) + sooner(value[2 * rows :])


TILE = 512
WIDE = BX * CH


def near_kernel(place_ref, mid_ref, near_ref, first_ref, second_ref, partial_ref, sum_ref, taps, hidden):
    samples = taps.shape[1]
    group = fill(taps, (mid_ref, near_ref))
    start_x = jnp.where(place_ref[1] % 2 == 0, BX, 0)
    first = first_ref[...]
    for line in range(BI + 2):
        keep = inside(place_ref, start_x, line)
        rows = slice(line * WIDE, (line + 1) * WIDE)
        for start in range(0, samples, TILE):
            lanes = slice(start, start + TILE)
            both = nn(first, taps[line * group : (line + 3) * group, lanes])
            hidden[rows, lanes] = jnp.where(keep, jax.nn.gelu(both[:WIDE]), 0.0).astype(BF)
            partial_ref[rows, lanes] = both[WIDE:]
    sum_ref[...] = joined(nn(second_ref[...], hidden[...]))


def far_kernel(place_ref, far_ref, partial_ref, sum_ref, first_ref, second_ref, out_ref, taps, hidden):
    samples = taps.shape[1]
    group = fill(taps, (far_ref,))
    start_x = jnp.where(place_ref[1] % 2 == 0, 0, BX)
    first = first_ref[...]
    for line in range(BI + 2):
        keep = inside(place_ref, start_x, line)
        rows = slice(line * WIDE, (line + 1) * WIDE)
        for start in range(0, samples, TILE):
            lanes = slice(start, start + TILE)
            value = nn(first, taps[line * group : (line + 3) * group, lanes]) + partial_ref[rows, lanes]
            hidden[rows, lanes] = jnp.where(keep, jax.nn.gelu(value), 0.0).astype(BF)
    total = joined(nn(second_ref[...], hidden[...])) + sum_ref[...]
    out_ref[...] = total.astype(BF).reshape(out_ref.shape)


def convolutions(place, mid, near, far, matrices):
    samples = mid.shape[1]
    first_near, first_far, second_near, second_far = matrices
    whole = pl.BlockSpec(memory_space=pltpu.VMEM)
    scalars = pl.BlockSpec(memory_space=pltpu.SMEM)
    tall = (BI + 4) * 3 * BX * CLASSES
    bins = (BI + 2) * WIDE
    partial, total = pl.pallas_call(
        near_kernel,
        in_specs=[scalars] + [whole] * 4,
        out_specs=(whole, whole),
        out_shape=(
            jax.ShapeDtypeStruct((bins, samples), F32),
            jax.ShapeDtypeStruct((CH * BI * BX, samples), F32),
        ),
        scratch_shapes=[pltpu.VMEM((2 * tall, samples), BF), pltpu.VMEM((bins, samples), BF)],
        compiler_params=pltpu.CompilerParams(vmem_limit_bytes=24 << 20),
        cost_estimate=pl.CostEstimate(flops=0, bytes_accessed=0, transcendentals=0),
        name="near",
    )(place, mid, near, first_near, second_near)
    return pl.pallas_call(
        far_kernel,
        in_specs=[scalars] + [whole] * 5,
        out_specs=whole,
        out_shape=jax.ShapeDtypeStruct((CH, BI, BX, samples), BF),
        scratch_shapes=[pltpu.VMEM((tall, samples), BF), pltpu.VMEM((bins, samples), BF)],
        compiler_params=pltpu.CompilerParams(vmem_limit_bytes=24 << 20),
        name="far",
    )(place, far, partial, total, first_far, second_far)


def first_matrices(kernel, odd):
    spatial = kernel.transpose(2, 3, 4, 1, 0)
    placed = [
        jnp.pad(spatial, ((0, 0), (at, BX + 1 - at), (0, 0), (0, 0), (0, 0))) for at in range(BX + 2)
    ]
    matrix = jnp.stack(placed, axis=0).transpose(0, 5, 1, 3, 2, 4)
    mirrored = jnp.concatenate([matrix[BX:], matrix[:BX]], axis=0)
    mirrored = jnp.concatenate(
        [mirrored[..., 2 * BX :, :], mirrored[..., BX : 2 * BX, :], mirrored[..., :BX, :]], axis=4
    )
    matrix = jnp.where(odd, mirrored, matrix)
    near = jnp.concatenate([matrix[BX:, ..., BX:, :], matrix[:BX, ..., BX:, :]], axis=0)
    far = matrix[:BX, ..., :BX, :]
    return near.reshape(2 * WIDE, -1), far.reshape(WIDE, -1)


def second_matrices(kernel, odd):
    spatial = kernel.transpose(2, 3, 4, 0, 1)
    placed = [
        [
            jnp.pad(spatial, ((i, BI - 1 - i), (x, BX - 1 - x), (0, 0), (0, 0), (0, 0)))
            for x in range(BX)
        ]
        for i in range(BI)
    ]
    matrix = jnp.stack([jnp.stack(line, axis=0) for line in placed], axis=0)
    matrix = matrix.transpose(4, 5, 0, 1, 2, 3, 6)
    low, high = matrix[..., :BX, :], matrix[..., BX:, :]
    rows = 3 * CH * BI * BX
    near, far = jnp.where(odd, low, high), jnp.where(odd, high, low)
    return near.reshape(rows, -1), far.reshape(rows, -1)


def swapped(block, axis, start):
    count = lax.axis_size(axis)
    pairs = [(i, i + 1) for i in range(start, count - 1, 2)]
    return lax.ppermute(block, axis, pairs + [(j, i) for i, j in pairs])


def per_device(traces, trace_dest, trace_bin, trace_class, band_weights, conv_first, conv_second):
    inline_size = lax.axis_size("inline")
    xline_size = lax.axis_size("xline")
    devices = inline_size * xline_size
    at_i, at_x = lax.axis_index("inline"), lax.axis_index("xline")
    count, samples = traces.shape
    width = samples // 2 + 128
    outgoing = pack(
        traces,
        trace_dest.reshape(1, count),
        trace_bin.reshape(1, count),
        trace_class.reshape(1, count),
        devices,
    )
    arrived = lax.all_to_all(
        outgoing.reshape(devices, 2 * CAP, width), ALL, split_axis=0, concat_axis=0, tiled=True
    ).reshape(devices * 2 * CAP, width)
    odd_i, odd_x = at_i % 2 == 1, at_x % 2 == 1
    matrices = first_matrices(conv_first, odd_x) + second_matrices(conv_second, odd_x)
    arrived, matrices = lax.optimization_barrier((arrived, matrices))
    volume = stack(arrived, band_weights)
    one, other = swapped(volume, "inline", 0), swapped(volume, "inline", 1)
    up, down = jnp.where(odd_i, one, other), jnp.where(odd_i, other, one)
    column = jnp.concatenate([up, volume, down], axis=0)
    far = swapped(column, "xline", 1)
    near = swapped(column, "xline", 0)
    place = jnp.stack(
        [at_i, at_x, jnp.int32(inline_size * BI), jnp.int32(xline_size * BX)]
    ).astype(jnp.int32)
    return convolutions(place, column, near, far, matrices)


def solution(mesh):
    return jax.shard_map(
        per_device,
        mesh=mesh,
        in_specs=(
            P(ALL, None),
            P(ALL, None),
            P(ALL),
            P(ALL),
            P(),
            P(),
            P(),
        ),
        out_specs=P(None, "inline", "xline", None),
        check_vma=False,
    )
```

```python
import jax
import jax.numpy as jnp
import numpy as np
from jax import lax
from jax.experimental import pallas as pl
from jax.experimental.pallas import tpu as pltpu
from jax.sharding import PartitionSpec as P

CLASSES = 8
BI = 2
BX = 2
CH = 32
CAP = 4
ALL = ("inline", "xline")
BF = jnp.bfloat16
F32 = jnp.float32
CELLS = CLASSES * BI * BX


def iota(shape, dim):
    return lax.broadcasted_iota(jnp.int32, shape, dim)


def nt(a, b):
    return lax.dot_general(a, b, (((1,), (1,)), ((), ())), preferred_element_type=F32)


def tn(a, b):
    return lax.dot_general(a, b, (((0,), (0,)), ((), ())), preferred_element_type=F32)


def nn(a, b):
    return jnp.dot(a, b, preferred_element_type=F32)


def before(count):
    return (iota((count, count), 0) < iota((count, count), 1)).astype(BF)


def pack_kernel(
    dest_ref, bin_ref, class_ref, traces_ref, out_ref, tags, loaded, packed, tag_sem, load_sem, store_sem
):
    rows, width = packed.shape
    count, half = loaded.shape[0] // 2, loaded.shape[1]
    devices = rows // (2 * CAP)
    parts = store_sem.shape[0]
    each = rows // parts
    small = []
    for number, ref in enumerate((dest_ref, bin_ref, class_ref)):
        small.append(pltpu.make_async_copy(ref, tags.at[number], tag_sem.at[number]))
        small[-1].start()
    loads = []
    for side in range(2):
        loads.append(
            pltpu.make_async_copy(
                traces_ref.at[:, pl.ds(side * half, half)],
                loaded.at[pl.ds(side * count, count)],
                load_sem.at[side],
            )
        )
        loads[-1].start()
    for copy in small:
        copy.wait()
    dest = tags[0]
    named = iota((devices, count), 0) == dest
    rank = nn(named.astype(BF), before(count))
    slot = jnp.sum(jnp.where(named, rank, 0.0), axis=0, keepdims=True)
    position = dest * (2 * CAP) + slot.astype(jnp.int32)
    cell = tags[1] * CLASSES + tags[2]
    lane = iota((128, count), 0)
    tagged = jnp.concatenate(
        [((lane == cell) | (lane == 127)).astype(BF), (lane == cell + CELLS).astype(BF)], axis=1
    )
    for load in loads:
        load.wait()
    stores = []
    for part in range(parts):
        piece = slice(part * each, (part + 1) * each)
        row = iota((each, count), 0) + part * each
        place = jnp.concatenate(
            [(row == position).astype(BF), (row == position + CAP).astype(BF)], axis=1
        )
        packed[piece, half:] = nt(place, tagged).astype(BF)
        packed[piece, :half] = nn(place, loaded[...]).astype(BF)
        chunk = pl.ds(part * each, each)
        stores.append(pltpu.make_async_copy(packed.at[chunk], out_ref.at[chunk], store_sem.at[part]))
        stores[-1].start()
    for copy in stores:
        copy.wait()


def pack(traces, dest, bins, classes, devices):
    count, samples = traces.shape
    rows, width = devices * 2 * CAP, samples // 2 + 128
    kept = pl.BlockSpec(memory_space=pltpu.HBM)
    pin = lambda array: pltpu.with_memory_space_constraint(array, pltpu.HBM)
    return pl.pallas_call(
        pack_kernel,
        in_specs=[kept] * 4,
        out_specs=kept,
        out_shape=pltpu.HBM((rows, width), BF),
        scratch_shapes=[
            pltpu.VMEM((3, 1, count), jnp.int32),
            pltpu.VMEM((2 * count, samples // 2), BF),
            pltpu.VMEM((rows, width), BF),
            pltpu.SemaphoreType.DMA((3,)),
            pltpu.SemaphoreType.DMA((2,)),
            pltpu.SemaphoreType.DMA((4,)),
        ],
        compiler_params=pltpu.CompilerParams(vmem_limit_bytes=24 << 20),
        name="pack",
    )(pin(dest), pin(bins), pin(classes), pin(traces))


def stack_kernel(arrived_ref, out_ref):
    width = arrived_ref.shape[1]
    half = width - 128
    stacked = tn(arrived_ref[:, half:], arrived_ref[...])
    fold = jnp.maximum(stacked[:CELLS, width - 1 : width], 1.0)
    out_ref[:, :half] = (stacked[:CELLS, :half] / fold).astype(BF)
    out_ref[:, half:] = (stacked[CELLS : 2 * CELLS, :half] / fold).astype(BF)


def stack(arrived):
    rows, width = arrived.shape
    whole = pl.BlockSpec(memory_space=pltpu.VMEM)
    return pl.pallas_call(
        stack_kernel,
        in_specs=[whole],
        out_specs=whole,
        out_shape=jax.ShapeDtypeStruct((CELLS, 2 * (width - 128)), BF),
        compiler_params=pltpu.CompilerParams(vmem_limit_bytes=12 << 20),
        name="stack",
    )(arrived)


BAND_PARTS = 8


def band_loads(source_ref, weights, sem):
    each = weights.shape[1] // BAND_PARTS
    loads = []
    for part in range(BAND_PARTS):
        blocks = pl.ds(part * each, each)
        loads.append(pltpu.make_async_copy(source_ref.at[:, blocks], weights.at[:, blocks], sem.at[part]))
        loads[-1].start()
    return loads


def move_out(averaged, weights, out, loads=None):
    rows = averaged.shape[0]
    classes, blocks, _, band = weights.shape
    kind = iota((rows, band), 0) % classes
    for block in range(blocks):
        if loads is not None and block % (blocks // BAND_PARTS) == 0:
            loads[block // (blocks // BAND_PARTS)].wait()
        start = block * band
        wide = jnp.concatenate([weights[number, block] for number in range(classes)], axis=1)
        moved = nn(averaged[:, start : start + 2 * band], wide)
        total = moved[:, :band]
        for number in range(1, classes):
            total = jnp.where(kind == number, moved[:, number * band : (number + 1) * band], total)
        out[:, start : start + band] = total.astype(BF)


def band_kernel(averaged_ref, band_ref, out_ref, weights, padded, sem):
    loads = band_loads(band_ref, weights, sem)
    rows, samples = averaged_ref.shape
    padded[:, :samples] = averaged_ref[...]
    padded[:, samples:] = jnp.zeros((rows, padded.shape[1] - samples), BF)
    move_out(padded, weights, out_ref, loads)


def moved_out(averaged, weights):
    rows, samples = averaged.shape
    whole = pl.BlockSpec(memory_space=pltpu.VMEM)
    return pl.pallas_call(
        band_kernel,
        in_specs=[whole, pl.BlockSpec(memory_space=pltpu.HBM)],
        out_specs=whole,
        out_shape=jax.ShapeDtypeStruct((rows, samples), BF),
        scratch_shapes=[
            pltpu.VMEM(weights.shape, BF),
            pltpu.VMEM((rows, samples + weights.shape[3]), BF),
            pltpu.SemaphoreType.DMA((BAND_PARTS,)),
        ],
        compiler_params=pltpu.CompilerParams(vmem_limit_bytes=16 << 20),
        name="band",
    )(averaged, pltpu.with_memory_space_constraint(weights, pltpu.HBM))


def later(value):
    rolled = pltpu.roll(value, 1, 1)
    return jnp.where(iota(value.shape, 1) == 0, jnp.zeros_like(rolled), rolled)


def sooner(value):
    samples = value.shape[1]
    rolled = pltpu.roll(value, samples - 1, 1)
    return jnp.where(iota(value.shape, 1) == samples - 1, jnp.zeros_like(rolled), rolled)


def fill(taps, columns, weights, padded, moved, loads=None):
    tall = BX * CLASSES
    group = 3 * len(columns) * tall
    samples = moved.shape[1]

    def place(value, first_line, which):
        for tap, shifted in enumerate((later(value), value, sooner(value))):
            for line in range(BI):
                at = (first_line + line) * group + (tap * len(columns) + which) * tall
                taps[at : at + tall, :] = shifted[line * tall : (line + 1) * tall]

    padded[:, samples:] = jnp.zeros((padded.shape[0], padded.shape[1] - samples), BF)
    for which, column in enumerate(columns):
        at = 2 * which * CELLS
        padded[at : at + CELLS, :samples] = column[:CELLS, :]
        padded[at + CELLS : at + 2 * CELLS, :samples] = column[2 * CELLS :, :]
        place(column[CELLS : 2 * CELLS, :], BI, which)
    move_out(padded, weights, moved, loads)
    for which in range(len(columns)):
        at = 2 * which * CELLS
        place(moved[at : at + CELLS, :], 0, which)
        place(moved[at + CELLS : at + 2 * CELLS, :], 2 * BI, which)
    return group


def inside(place_ref, start_x, line):
    bin_x = iota((BX * CH, 1), 0) // CH + start_x + place_ref[1] * BX - 1
    bin_i = line + place_ref[0] * BI - 1
    return (bin_x >= 0) & (bin_x < place_ref[3]) & (bin_i >= 0) & (bin_i < place_ref[2])


def joined(value):
    rows = value.shape[0] // 3
    return value[rows : 2 * rows] + later(value[:rows]) + sooner(value[2 * rows :])


TILE = 512
WIDE = BX * CH


def near_kernel(
    place_ref, band_ref, mid_ref, near_ref, first_ref, second_ref,
    partial_ref, sum_ref, weights, taps, hidden, padded, moved, sem,
):
    samples = taps.shape[1]
    loads = band_loads(band_ref, weights, sem)
    group = fill(taps, (mid_ref, near_ref), weights, padded, moved, loads)
    start_x = jnp.where(place_ref[1] % 2 == 0, BX, 0)
    first = first_ref[...]
    for line in range(BI + 2):
        keep = inside(place_ref, start_x, line)
        rows = slice(line * WIDE, (line + 1) * WIDE)
        for start in range(0, samples, TILE):
            lanes = slice(start, start + TILE)
            both = nn(first, taps[line * group : (line + 3) * group, lanes])
            hidden[rows, lanes] = jnp.where(keep, jax.nn.gelu(both[:WIDE]), 0.0).astype(BF)
            partial_ref[rows, lanes] = both[WIDE:]
    sum_ref[...] = joined(nn(second_ref[...], hidden[...]))


def far_kernel(
    place_ref, weights, far_ref, partial_ref, sum_ref, first_ref, second_ref, out_ref, taps, hidden, padded, moved
):
    samples = taps.shape[1]
    group = fill(taps, (far_ref,), weights, padded, moved)
    start_x = jnp.where(place_ref[1] % 2 == 0, 0, BX)
    first = first_ref[...]
    for line in range(BI + 2):
        keep = inside(place_ref, start_x, line)
        rows = slice(line * WIDE, (line + 1) * WIDE)
        for start in range(0, samples, TILE):
            lanes = slice(start, start + TILE)
            value = nn(first, taps[line * group : (line + 3) * group, lanes]) + partial_ref[rows, lanes]
            hidden[rows, lanes] = jnp.where(keep, jax.nn.gelu(value), 0.0).astype(BF)
    held = hidden[...]
    total = nn(second_ref[...], jnp.concatenate([later(held), held, sooner(held)], axis=0)) + sum_ref[...]
    out_ref[...] = total.astype(BF).reshape(out_ref.shape)


def convolutions(place, weights, mid, near, far, matrices):
    samples = mid.shape[1]
    first_near, first_far, second_near, second_far = matrices
    whole = pl.BlockSpec(memory_space=pltpu.VMEM)
    scalars = pl.BlockSpec(memory_space=pltpu.SMEM)
    tall = (BI + 4) * 3 * BX * CLASSES
    bins = (BI + 2) * WIDE
    longer = samples + weights.shape[3]
    partial, total, held = pl.pallas_call(
        near_kernel,
        in_specs=[scalars, pl.BlockSpec(memory_space=pltpu.HBM)] + [whole] * 4,
        out_specs=(whole, whole, whole),
        out_shape=(
            jax.ShapeDtypeStruct((bins, samples), F32),
            jax.ShapeDtypeStruct((CH * BI * BX, samples), F32),
            jax.ShapeDtypeStruct(weights.shape, BF),
        ),
        scratch_shapes=[
            pltpu.VMEM((2 * tall, samples), BF),
            pltpu.VMEM((bins, samples), BF),
            pltpu.VMEM((4 * CELLS, longer), BF),
            pltpu.VMEM((4 * CELLS, samples), BF),
            pltpu.SemaphoreType.DMA((BAND_PARTS,)),
        ],
        compiler_params=pltpu.CompilerParams(vmem_limit_bytes=24 << 20),
        name="near",
    )(place, pltpu.with_memory_space_constraint(weights, pltpu.HBM), mid, near, first_near, second_near)
    return pl.pallas_call(
        far_kernel,
        in_specs=[scalars] + [whole] * 6,
        out_specs=whole,
        out_shape=jax.ShapeDtypeStruct((CH, BI, BX, samples), BF),
        scratch_shapes=[
            pltpu.VMEM((tall, samples), BF),
            pltpu.VMEM((bins, samples), BF),
            pltpu.VMEM((2 * CELLS, longer), BF),
            pltpu.VMEM((2 * CELLS, samples), BF),
        ],
        compiler_params=pltpu.CompilerParams(vmem_limit_bytes=24 << 20),
        name="far",
    )(place, held, far, partial, total, first_far, second_far)


def first_matrices(kernel, odd):
    spatial = kernel.transpose(2, 3, 4, 1, 0)
    placed = [
        jnp.pad(spatial, ((0, 0), (at, BX + 1 - at), (0, 0), (0, 0), (0, 0))) for at in range(BX + 2)
    ]
    matrix = jnp.stack(placed, axis=0).transpose(0, 5, 1, 3, 2, 4)
    mirrored = jnp.concatenate([matrix[BX:], matrix[:BX]], axis=0)
    mirrored = jnp.concatenate(
        [mirrored[..., 2 * BX :, :], mirrored[..., BX : 2 * BX, :], mirrored[..., :BX, :]], axis=4
    )
    matrix = jnp.where(odd, mirrored, matrix)
    near = jnp.concatenate([matrix[BX:, ..., BX:, :], matrix[:BX, ..., BX:, :]], axis=0)
    far = matrix[:BX, ..., :BX, :]
    return near.reshape(2 * WIDE, -1), far.reshape(WIDE, -1)


def second_matrices(kernel, odd):
    spatial = kernel.transpose(2, 3, 4, 0, 1)
    placed = [
        [
            jnp.pad(spatial, ((i, BI - 1 - i), (x, BX - 1 - x), (0, 0), (0, 0), (0, 0)))
            for x in range(BX)
        ]
        for i in range(BI)
    ]
    matrix = jnp.stack([jnp.stack(line, axis=0) for line in placed], axis=0)
    matrix = matrix.transpose(4, 5, 0, 1, 2, 3, 6)
    low, high = matrix[..., :BX, :], matrix[..., BX:, :]
    rows = 3 * CH * BI * BX
    near, far = jnp.where(odd, low, high), jnp.where(odd, high, low)
    far = jnp.moveaxis(far, 0, 3)
    return near.reshape(rows, -1), far.reshape(rows // 3, -1)


def swapped(block, axis, start):
    count = lax.axis_size(axis)
    pairs = [(i, i + 1) for i in range(start, count - 1, 2)]
    return lax.ppermute(block, axis, pairs + [(j, i) for i, j in pairs])


def per_device(traces, trace_dest, trace_bin, trace_class, band_weights, conv_first, conv_second):
    inline_size = lax.axis_size("inline")
    xline_size = lax.axis_size("xline")
    devices = inline_size * xline_size
    at_i, at_x = lax.axis_index("inline"), lax.axis_index("xline")
    count, samples = traces.shape
    width = samples // 2 + 128
    outgoing = pack(
        traces,
        trace_dest.reshape(1, count),
        trace_bin.reshape(1, count),
        trace_class.reshape(1, count),
        devices,
    )
    arrived = lax.all_to_all(
        outgoing.reshape(devices, 2 * CAP, width), ALL, split_axis=0, concat_axis=0, tiled=True
    ).reshape(devices * 2 * CAP, width)
    odd_i, odd_x = at_i % 2 == 1, at_x % 2 == 1
    matrices = first_matrices(conv_first, odd_x) + second_matrices(conv_second, odd_x)
    arrived, matrices = lax.optimization_barrier((arrived, matrices))
    classes, blocks, steps, band, _ = band_weights.shape
    weights = band_weights.reshape(classes, blocks, steps * band, band)
    averaged = stack(arrived)
    one, other = swapped(averaged, "inline", 0), swapped(averaged, "inline", 1)
    volume = moved_out(averaged, weights)
    up, down = jnp.where(odd_i, one, other), jnp.where(odd_i, other, one)
    column = jnp.concatenate([up, volume, down], axis=0)
    far = swapped(column, "xline", 1)
    near = swapped(column, "xline", 0)
    place = jnp.stack(
        [at_i, at_x, jnp.int32(inline_size * BI), jnp.int32(xline_size * BX)]
    ).astype(jnp.int32)
    return convolutions(place, weights, column, near, far, matrices)


def solution(mesh):
    return jax.shard_map(
        per_device,
        mesh=mesh,
        in_specs=(
            P(ALL, None),
            P(ALL, None),
            P(ALL),
            P(ALL),
            P(),
            P(),
            P(),
        ),
        out_specs=P(None, "inline", "xline", None),
        check_vma=False,
    )
```

```python
import jax
import jax.numpy as jnp
import numpy as np
from jax import lax
from jax.experimental import pallas as pl
from jax.experimental.pallas import tpu as pltpu
from jax.sharding import PartitionSpec as P

CLASSES = 8
BI = 2
BX = 2
CH = 32
CAP = 4
ALL = ("inline", "xline")
BF = jnp.bfloat16
F32 = jnp.float32
CELLS = CLASSES * BI * BX


def iota(shape, dim):
    return lax.broadcasted_iota(jnp.int32, shape, dim)


def nt(a, b):
    return lax.dot_general(a, b, (((1,), (1,)), ((), ())), preferred_element_type=F32)


def tn(a, b):
    return lax.dot_general(a, b, (((0,), (0,)), ((), ())), preferred_element_type=F32)


def nn(a, b):
    return jnp.dot(a, b, preferred_element_type=F32)


def before(count):
    return (iota((count, count), 0) < iota((count, count), 1)).astype(BF)


def pack_kernel(
    dest_ref, bin_ref, class_ref, traces_ref, out_ref, tags, loaded, packed, tag_sem, load_sem, store_sem
):
    rows, width = packed.shape
    count, half = loaded.shape[0] // 2, loaded.shape[1]
    devices = rows // (2 * CAP)
    parts = store_sem.shape[0]
    each = rows // parts
    small = []
    for number, ref in enumerate((dest_ref, bin_ref, class_ref)):
        small.append(pltpu.make_async_copy(ref, tags.at[number], tag_sem.at[number]))
        small[-1].start()
    loads = []
    for side in range(2):
        loads.append(
            pltpu.make_async_copy(
                traces_ref.at[:, pl.ds(side * half, half)],
                loaded.at[pl.ds(side * count, count)],
                load_sem.at[side],
            )
        )
        loads[-1].start()
    for copy in small:
        copy.wait()
    dest = tags[0]
    named = iota((devices, count), 0) == dest
    rank = nn(named.astype(BF), before(count))
    slot = jnp.sum(jnp.where(named, rank, 0.0), axis=0, keepdims=True)
    position = dest * (2 * CAP) + slot.astype(jnp.int32)
    cell = tags[1] * CLASSES + tags[2]
    lane = iota((128, count), 0)
    tagged = jnp.concatenate(
        [((lane == cell) | (lane == 127)).astype(BF), (lane == cell + CELLS).astype(BF)], axis=1
    )
    for load in loads:
        load.wait()
    stores = []
    for part in range(parts):
        piece = slice(part * each, (part + 1) * each)
        row = iota((each, count), 0) + part * each
        place = jnp.concatenate(
            [(row == position).astype(BF), (row == position + CAP).astype(BF)], axis=1
        )
        packed[piece, half:] = nt(place, tagged).astype(BF)
        packed[piece, :half] = nn(place, loaded[...]).astype(BF)
        chunk = pl.ds(part * each, each)
        stores.append(pltpu.make_async_copy(packed.at[chunk], out_ref.at[chunk], store_sem.at[part]))
        stores[-1].start()
    for copy in stores:
        copy.wait()


def pack(traces, dest, bins, classes, devices):
    count, samples = traces.shape
    rows, width = devices * 2 * CAP, samples // 2 + 128
    kept = pl.BlockSpec(memory_space=pltpu.HBM)
    pin = lambda array: pltpu.with_memory_space_constraint(array, pltpu.HBM)
    return pl.pallas_call(
        pack_kernel,
        in_specs=[kept] * 4,
        out_specs=kept,
        out_shape=pltpu.HBM((rows, width), BF),
        scratch_shapes=[
            pltpu.VMEM((3, 1, count), jnp.int32),
            pltpu.VMEM((2 * count, samples // 2), BF),
            pltpu.VMEM((rows, width), BF),
            pltpu.SemaphoreType.DMA((3,)),
            pltpu.SemaphoreType.DMA((2,)),
            pltpu.SemaphoreType.DMA((4,)),
        ],
        compiler_params=pltpu.CompilerParams(vmem_limit_bytes=24 << 20),
        name="pack",
    )(pin(dest), pin(bins), pin(classes), pin(traces))


def stack_kernel(arrived_ref, out_ref):
    width = arrived_ref.shape[1]
    half = width - 128
    stacked = tn(arrived_ref[:, half:], arrived_ref[...])
    fold = jnp.maximum(stacked[:CELLS, width - 1 : width], 1.0)
    out_ref[:, :half] = (stacked[:CELLS, :half] / fold).astype(BF)
    out_ref[:, half:] = (stacked[CELLS : 2 * CELLS, :half] / fold).astype(BF)


def stack(arrived):
    rows, width = arrived.shape
    whole = pl.BlockSpec(memory_space=pltpu.VMEM)
    return pl.pallas_call(
        stack_kernel,
        in_specs=[whole],
        out_specs=whole,
        out_shape=jax.ShapeDtypeStruct((CELLS, 2 * (width - 128)), BF),
        compiler_params=pltpu.CompilerParams(vmem_limit_bytes=12 << 20),
        name="stack",
    )(arrived)


def band_loads(source_ref, weights, sem, sizes):
    loads, first = {}, 0
    for number, size in enumerate(sizes):
        blocks = pl.ds(first, size)
        loads[first] = pltpu.make_async_copy(source_ref.at[:, blocks], weights.at[:, blocks], sem.at[number])
        loads[first].start()
        first += size
    return loads


def moved_block(averaged, weights, block, loads):
    if block in loads:
        loads[block].wait()
    classes, _, _, band = weights.shape
    start = block * band
    wide = jnp.concatenate([weights[number, block] for number in range(classes)], axis=1)
    moved = nn(averaged[:, start : start + 2 * band], wide)
    kind = iota((averaged.shape[0], band), 0) % classes
    total = moved[:, :band]
    for number in range(1, classes):
        total = jnp.where(kind == number, moved[:, number * band : (number + 1) * band], total)
    return total.astype(BF)


BAND_SIZES = (2, 2, 2, 2, 2, 2, 2, 2)
NEAR_SIZES = (2, 2, 2, 2, 2, 2, 2, 2)


def band_kernel(averaged_ref, band_ref, out_ref, weights, padded, sem):
    loads = band_loads(band_ref, weights, sem, BAND_SIZES)
    rows, samples = averaged_ref.shape
    band = weights.shape[3]
    padded[:, :samples] = averaged_ref[...]
    padded[:, samples:] = jnp.zeros((rows, band), BF)
    for block in range(weights.shape[1]):
        out_ref[:, block * band : (block + 1) * band] = moved_block(padded, weights, block, loads)


def moved_out(averaged, weights):
    rows, samples = averaged.shape
    whole = pl.BlockSpec(memory_space=pltpu.VMEM)
    return pl.pallas_call(
        band_kernel,
        in_specs=[whole, pl.BlockSpec(memory_space=pltpu.HBM)],
        out_specs=whole,
        out_shape=jax.ShapeDtypeStruct((rows, samples), BF),
        scratch_shapes=[
            pltpu.VMEM(weights.shape, BF),
            pltpu.VMEM((rows, samples + weights.shape[3]), BF),
            pltpu.SemaphoreType.DMA((len(BAND_SIZES),)),
        ],
        compiler_params=pltpu.CompilerParams(vmem_limit_bytes=16 << 20),
        name="band",
    )(averaged, pltpu.with_memory_space_constraint(weights, pltpu.HBM))


TILE = 2048
WIDE = BX * CH
EDGE = 128
ALL_LINES = BI + 4
TALL = BX * CLASSES


def taps_of(padded, rows, start):
    window = padded[rows, start : start + TILE + 2 * EDGE]
    inner = slice(EDGE, EDGE + TILE)
    width = window.shape[1]
    return pltpu.roll(window, 1, 1)[:, inner], window[:, inner], pltpu.roll(window, width - 1, 1)[:, inner]


def clear_edges(padded):
    zeros = jnp.zeros((padded.shape[0], EDGE), BF)
    padded[:, :EDGE] = zeros
    padded[:, padded.shape[1] - EDGE :] = zeros


def inside(place_ref, start_x, line):
    bin_x = iota((WIDE, 1), 0) // CH + start_x + place_ref[1] * BX - 1
    bin_i = line + place_ref[0] * BI - 1
    return (bin_x >= 0) & (bin_x < place_ref[3]) & (bin_i >= 0) & (bin_i < place_ref[2])


def run_tiles(
    columns, weights, loads, first, second, keeps, split, store, averaged, volume, taps, hidden
):
    samples = volume.shape[1] - 2 * EDGE
    _, blocks, _, band = weights.shape
    count = len(columns)
    group = 3 * count * TALL
    clear_edges(volume)
    clear_edges(hidden)
    averaged[:, samples:] = jnp.zeros((averaged.shape[0], averaged.shape[1] - samples), BF)
    for which, column in enumerate(columns):
        at = 2 * which * CELLS
        averaged[at : at + CELLS, :samples] = column[:CELLS, :]
        averaged[at + CELLS : at + 2 * CELLS, :samples] = column[2 * CELLS : 3 * CELLS, :]
        at = (3 * which + 1) * CELLS
        volume[at : at + CELLS, EDGE : EDGE + samples] = column[CELLS : 2 * CELLS, :]

    def move_out(block):
        total = moved_block(averaged, weights, block, loads)
        start = block * band
        lanes = slice(EDGE + start, EDGE + start + band)
        for which in range(count):
            volume[3 * which * CELLS : (3 * which + 1) * CELLS, lanes] = total[
                2 * which * CELLS : (2 * which + 1) * CELLS
            ]
            volume[(3 * which + 2) * CELLS : (3 * which + 3) * CELLS, lanes] = total[
                (2 * which + 1) * CELLS : (2 * which + 2) * CELLS
            ]

    def first_convolution(start):
        lanes = slice(start, start + TILE)
        for which in range(count):
            rows = slice(3 * which * CELLS, 3 * (which + 1) * CELLS)
            for tap, value in enumerate(taps_of(volume, rows, start)):
                for line in range(ALL_LINES):
                    at = line * group + (tap * count + which) * TALL
                    taps[at : at + TALL, lanes] = value[line * TALL : (line + 1) * TALL]
        for line in range(BI + 2):
            rows = slice(line * WIDE, (line + 1) * WIDE)
            value = split(nn(first, taps[line * group : (line + 3) * group, lanes]), rows, lanes)
            value = jnp.where(keeps[line], jax.nn.gelu(value), 0.0).astype(BF)
            hidden[rows, EDGE + start : EDGE + start + TILE] = value

    def second_convolution(start):
        held = jnp.concatenate(taps_of(hidden, slice(None), start), axis=0)
        store(nn(second, held), slice(start, start + TILE))

    done = 0
    for start in range(0, samples, TILE):
        ready = min((start + TILE) // band + 1, blocks)
        for block in range(done, ready):
            move_out(block)
        done = ready
        first_convolution(start)
        if start:
            second_convolution(start - TILE)
    second_convolution(samples - TILE)


def near_kernel(
    place_ref, band_ref, mid_ref, near_ref, first_ref, second_ref,
    partial_ref, sum_ref, weights, averaged, volume, taps, hidden, sem,
):
    loads = band_loads(band_ref, weights, sem, NEAR_SIZES)
    start_x = jnp.where(place_ref[1] % 2 == 0, BX, 0)
    keeps = [inside(place_ref, start_x, line) for line in range(BI + 2)]

    def split(both, rows, lanes):
        partial_ref[rows, lanes] = both[WIDE:]
        return both[:WIDE]

    def store(value, lanes):
        sum_ref[:, lanes] = value

    run_tiles(
        (mid_ref, near_ref), weights, loads, first_ref[...], second_ref[...], keeps, split, store,
        averaged, volume, taps, hidden,
    )


def far_kernel(
    place_ref, weights, far_ref, partial_ref, sum_ref, first_ref, second_ref, out_ref,
    averaged, volume, taps, hidden,
):
    start_x = jnp.where(place_ref[1] % 2 == 0, 0, BX)
    keeps = [inside(place_ref, start_x, line) for line in range(BI + 2)]

    def split(value, rows, lanes):
        return value + partial_ref[rows, lanes]

    def store(value, lanes):
        total = (value + sum_ref[:, lanes]).astype(BF)
        out_ref[:, :, :, lanes] = total.reshape(out_ref.shape[:3] + (TILE,))

    run_tiles(
        (far_ref,), weights, {}, first_ref[...], second_ref[...], keeps, split, store,
        averaged, volume, taps, hidden,
    )


def convolutions(place, weights, mid, near, far, matrices):
    samples = mid.shape[1]
    first_near, first_far, second_near, second_far = matrices
    whole = pl.BlockSpec(memory_space=pltpu.VMEM)
    scalars = pl.BlockSpec(memory_space=pltpu.SMEM)
    bins = (BI + 2) * WIDE

    def buffers(count):
        return [
            pltpu.VMEM((2 * count * CELLS, samples + weights.shape[3]), BF),
            pltpu.VMEM((3 * count * CELLS, samples + 2 * EDGE), BF),
            pltpu.VMEM((3 * count * ALL_LINES * TALL, samples), BF),
            pltpu.VMEM((bins, samples + 2 * EDGE), BF),
        ]

    partial, total, held = pl.pallas_call(
        near_kernel,
        in_specs=[scalars, pl.BlockSpec(memory_space=pltpu.HBM)] + [whole] * 4,
        out_specs=(whole, whole, whole),
        out_shape=(
            jax.ShapeDtypeStruct((bins, samples), F32),
            jax.ShapeDtypeStruct((CH * BI * BX, samples), F32),
            jax.ShapeDtypeStruct(weights.shape, BF),
        ),
        scratch_shapes=buffers(2) + [pltpu.SemaphoreType.DMA((len(NEAR_SIZES),))],
        compiler_params=pltpu.CompilerParams(vmem_limit_bytes=24 << 20),
        cost_estimate=pl.CostEstimate(flops=0, bytes_accessed=0, transcendentals=0),
        name="near",
    )(place, pltpu.with_memory_space_constraint(weights, pltpu.HBM), mid, near, first_near, second_near)
    return pl.pallas_call(
        far_kernel,
        in_specs=[scalars] + [whole] * 6,
        out_specs=whole,
        out_shape=jax.ShapeDtypeStruct((CH, BI, BX, samples), BF),
        scratch_shapes=buffers(1),
        compiler_params=pltpu.CompilerParams(vmem_limit_bytes=24 << 20),
        name="far",
    )(place, held, far, partial, total, first_far, second_far)


def first_matrices(kernel, odd):
    spatial = kernel.transpose(2, 3, 4, 1, 0)
    placed = [
        jnp.pad(spatial, ((0, 0), (at, BX + 1 - at), (0, 0), (0, 0), (0, 0))) for at in range(BX + 2)
    ]
    matrix = jnp.stack(placed, axis=0).transpose(0, 5, 1, 3, 2, 4)
    mirrored = jnp.concatenate([matrix[BX:], matrix[:BX]], axis=0)
    mirrored = jnp.concatenate(
        [mirrored[..., 2 * BX :, :], mirrored[..., BX : 2 * BX, :], mirrored[..., :BX, :]], axis=4
    )
    matrix = jnp.where(odd, mirrored, matrix)
    near = jnp.concatenate([matrix[BX:, ..., BX:, :], matrix[:BX, ..., BX:, :]], axis=0)
    far = matrix[:BX, ..., :BX, :]
    return near.reshape(2 * WIDE, -1), far.reshape(WIDE, -1)


def second_matrices(kernel, odd):
    spatial = kernel.transpose(2, 3, 4, 0, 1)
    placed = [
        [
            jnp.pad(spatial, ((i, BI - 1 - i), (x, BX - 1 - x), (0, 0), (0, 0), (0, 0)))
            for x in range(BX)
        ]
        for i in range(BI)
    ]
    matrix = jnp.stack([jnp.stack(line, axis=0) for line in placed], axis=0)
    matrix = matrix.transpose(4, 5, 0, 1, 2, 3, 6)
    low, high = matrix[..., :BX, :], matrix[..., BX:, :]
    rows = CH * BI * BX
    near, far = jnp.where(odd, low, high), jnp.where(odd, high, low)
    return tuple(jnp.moveaxis(side, 0, 3).reshape(rows, -1) for side in (near, far))


def swapped(block, axis, start):
    count = lax.axis_size(axis)
    pairs = [(i, i + 1) for i in range(start, count - 1, 2)]
    return lax.ppermute(block, axis, pairs + [(j, i) for i, j in pairs])


def per_device(traces, trace_dest, trace_bin, trace_class, band_weights, conv_first, conv_second):
    inline_size = lax.axis_size("inline")
    xline_size = lax.axis_size("xline")
    devices = inline_size * xline_size
    at_i, at_x = lax.axis_index("inline"), lax.axis_index("xline")
    count, samples = traces.shape
    width = samples // 2 + 128
    outgoing = pack(
        traces,
        trace_dest.reshape(1, count),
        trace_bin.reshape(1, count),
        trace_class.reshape(1, count),
        devices,
    )
    arrived = lax.all_to_all(
        outgoing.reshape(devices, 2 * CAP, width), ALL, split_axis=0, concat_axis=0, tiled=True
    ).reshape(devices * 2 * CAP, width)
    odd_i, odd_x = at_i % 2 == 1, at_x % 2 == 1
    matrices = first_matrices(conv_first, odd_x) + second_matrices(conv_second, odd_x)
    arrived, matrices = lax.optimization_barrier((arrived, matrices))
    classes, blocks, steps, band, _ = band_weights.shape
    weights = band_weights.reshape(classes, blocks, steps * band, band)
    averaged = stack(arrived)
    one, other = swapped(averaged, "inline", 0), swapped(averaged, "inline", 1)
    volume = moved_out(averaged, weights)
    up, down = jnp.where(odd_i, one, other), jnp.where(odd_i, other, one)
    column = jnp.concatenate([up, volume, down], axis=0)
    sent = jnp.concatenate([up, volume, down, up[:16]], axis=0)
    far = swapped(sent, "xline", 1)
    near = swapped(column, "xline", 0)
    place = jnp.stack(
        [at_i, at_x, jnp.int32(inline_size * BI), jnp.int32(xline_size * BX)]
    ).astype(jnp.int32)
    return convolutions(place, weights, column, near, far, matrices)


def solution(mesh):
    return jax.shard_map(
        per_device,
        mesh=mesh,
        in_specs=(
            P(ALL, None),
            P(ALL, None),
            P(ALL),
            P(ALL),
            P(),
            P(),
            P(),
        ),
        out_specs=P(None, "inline", "xline", None),
        check_vma=False,
    )
```

```python
import jax
import jax.numpy as jnp
import numpy as np
from jax import lax
from jax.experimental import pallas as pl
from jax.experimental.pallas import tpu as pltpu
from jax.sharding import PartitionSpec as P

CLASSES = 8
BI = 2
BX = 2
CH = 32
CAP = 4
ALL = ("inline", "xline")
BF = jnp.bfloat16
F32 = jnp.float32
CELLS = CLASSES * BI * BX


def iota(shape, dim):
    return lax.broadcasted_iota(jnp.int32, shape, dim)


def nt(a, b):
    return lax.dot_general(a, b, (((1,), (1,)), ((), ())), preferred_element_type=F32)


def tn(a, b):
    return lax.dot_general(a, b, (((0,), (0,)), ((), ())), preferred_element_type=F32)


def nn(a, b):
    return jnp.dot(a, b, preferred_element_type=F32)


def before(count):
    return (iota((count, count), 0) < iota((count, count), 1)).astype(BF)


def pack_kernel(
    dest_ref, bin_ref, class_ref, traces_ref, out_ref, tags, loaded, packed, tag_sem, load_sem, store_sem
):
    rows, width = packed.shape
    count, half = loaded.shape[0] // 2, loaded.shape[1]
    devices = rows // (2 * CAP)
    parts = store_sem.shape[0]
    each = rows // parts
    small = []
    for number, ref in enumerate((dest_ref, bin_ref, class_ref)):
        small.append(pltpu.make_async_copy(ref, tags.at[number], tag_sem.at[number]))
        small[-1].start()
    loads = []
    for side in range(2):
        loads.append(
            pltpu.make_async_copy(
                traces_ref.at[:, pl.ds(side * half, half)],
                loaded.at[pl.ds(side * count, count)],
                load_sem.at[side],
            )
        )
        loads[-1].start()
    for copy in small:
        copy.wait()
    dest = tags[0]
    named = iota((devices, count), 0) == dest
    rank = nn(named.astype(BF), before(count))
    slot = jnp.sum(jnp.where(named, rank, 0.0), axis=0, keepdims=True)
    position = dest * (2 * CAP) + slot.astype(jnp.int32)
    cell = tags[1] * CLASSES + tags[2]
    lane = iota((128, count), 0)
    tagged = jnp.concatenate(
        [((lane == cell) | (lane == 127)).astype(BF), (lane == cell + CELLS).astype(BF)], axis=1
    )
    for load in loads:
        load.wait()
    stores = []
    for part in range(parts):
        piece = slice(part * each, (part + 1) * each)
        row = iota((each, count), 0) + part * each
        place = jnp.concatenate(
            [(row == position).astype(BF), (row == position + CAP).astype(BF)], axis=1
        )
        packed[piece, half:] = nt(place, tagged).astype(BF)
        packed[piece, :half] = nn(place, loaded[...]).astype(BF)
        chunk = pl.ds(part * each, each)
        stores.append(pltpu.make_async_copy(packed.at[chunk], out_ref.at[chunk], store_sem.at[part]))
        stores[-1].start()
    for copy in stores:
        copy.wait()


def pack(traces, dest, bins, classes, devices):
    count, samples = traces.shape
    rows, width = devices * 2 * CAP, samples // 2 + 128
    kept = pl.BlockSpec(memory_space=pltpu.HBM)
    pin = lambda array: pltpu.with_memory_space_constraint(array, pltpu.HBM)
    return pl.pallas_call(
        pack_kernel,
        in_specs=[kept] * 4,
        out_specs=kept,
        out_shape=pltpu.HBM((rows, width), BF),
        scratch_shapes=[
            pltpu.VMEM((3, 1, count), jnp.int32),
            pltpu.VMEM((2 * count, samples // 2), BF),
            pltpu.VMEM((rows, width), BF),
            pltpu.SemaphoreType.DMA((3,)),
            pltpu.SemaphoreType.DMA((2,)),
            pltpu.SemaphoreType.DMA((4,)),
        ],
        compiler_params=pltpu.CompilerParams(vmem_limit_bytes=24 << 20),
        name="pack",
    )(pin(dest), pin(bins), pin(classes), pin(traces))


def stack_kernel(arrived_ref, out_ref):
    width = arrived_ref.shape[1]
    half = width - 128
    stacked = tn(arrived_ref[:, half:], arrived_ref[...])
    fold = jnp.maximum(stacked[:CELLS, width - 1 : width], 1.0)
    out_ref[:, :half] = (stacked[:CELLS, :half] / fold).astype(BF)
    out_ref[:, half:] = (stacked[CELLS : 2 * CELLS, :half] / fold).astype(BF)


def stack(arrived):
    rows, width = arrived.shape
    whole = pl.BlockSpec(memory_space=pltpu.VMEM)
    return pl.pallas_call(
        stack_kernel,
        in_specs=[whole],
        out_specs=whole,
        out_shape=jax.ShapeDtypeStruct((CELLS, 2 * (width - 128)), BF),
        compiler_params=pltpu.CompilerParams(vmem_limit_bytes=12 << 20),
        name="stack",
    )(arrived)


def band_loads(source_ref, weights, sem, sizes):
    loads, first = {}, 0
    for number, size in enumerate(sizes):
        blocks = pl.ds(first, size)
        loads[first] = pltpu.make_async_copy(source_ref.at[:, blocks], weights.at[:, blocks], sem.at[number])
        loads[first].start()
        first += size
    return loads


def moved_block(averaged, weights, block, loads):
    if block in loads:
        loads[block].wait()
    classes, _, _, band = weights.shape
    start = block * band
    wide = jnp.concatenate([weights[number, block] for number in range(classes)], axis=1)
    moved = nn(averaged[:, start : start + 2 * band], wide)
    kind = iota((averaged.shape[0], band), 0) % classes
    total = moved[:, :band]
    for number in range(1, classes):
        total = jnp.where(kind == number, moved[:, number * band : (number + 1) * band], total)
    return total.astype(BF)


BAND_SIZES = (2, 2, 2, 2, 2, 2, 2, 2)


def band_kernel(averaged_ref, band_ref, out_ref, weights, padded, sem):
    loads = band_loads(band_ref, weights, sem, BAND_SIZES)
    rows, samples = averaged_ref.shape
    band = weights.shape[3]
    padded[:, :samples] = averaged_ref[...]
    padded[:, samples:] = jnp.zeros((rows, band), BF)
    for block in range(weights.shape[1]):
        out_ref[:, block * band : (block + 1) * band] = moved_block(padded, weights, block, loads)


def moved_out(averaged, weights):
    rows, samples = averaged.shape
    whole = pl.BlockSpec(memory_space=pltpu.VMEM)
    return pl.pallas_call(
        band_kernel,
        in_specs=[whole, pl.BlockSpec(memory_space=pltpu.HBM)],
        out_specs=(whole, whole),
        out_shape=(jax.ShapeDtypeStruct((rows, samples), BF), jax.ShapeDtypeStruct(weights.shape, BF)),
        scratch_shapes=[
            pltpu.VMEM((rows, samples + weights.shape[3]), BF),
            pltpu.SemaphoreType.DMA((len(BAND_SIZES),)),
        ],
        compiler_params=pltpu.CompilerParams(vmem_limit_bytes=16 << 20),
        name="band",
    )(averaged, pltpu.with_memory_space_constraint(weights, pltpu.HBM))


def border_kernel(place_ref, one_ref, other_ref, own_ref, weights, column_ref, sent_ref, padded):
    samples = own_ref.shape[1]
    band = weights.shape[3]
    odd = place_ref[0] % 2 == 1
    one, other = one_ref[...], other_ref[...]
    padded[:CELLS, :samples] = jnp.where(odd, one, other)
    padded[CELLS:, :samples] = jnp.where(odd, other, one)
    padded[:, samples:] = jnp.zeros((2 * CELLS, band), BF)
    own = own_ref[...]
    column_ref[CELLS : 2 * CELLS, :] = own
    sent_ref[CELLS : 2 * CELLS, :] = own
    sent_ref[3 * CELLS :, :] = own[: sent_ref.shape[0] - 3 * CELLS]
    for block in range(weights.shape[1]):
        lanes = slice(block * band, (block + 1) * band)
        total = moved_block(padded, weights, block, {})
        for ref in (column_ref, sent_ref):
            ref[:CELLS, lanes] = total[:CELLS]
            ref[2 * CELLS : 3 * CELLS, lanes] = total[CELLS:]


def border(place, one, other, own, weights):
    samples = own.shape[1]
    whole = pl.BlockSpec(memory_space=pltpu.VMEM)
    return pl.pallas_call(
        border_kernel,
        in_specs=[pl.BlockSpec(memory_space=pltpu.SMEM)] + [whole] * 4,
        out_specs=(whole, whole),
        out_shape=(
            jax.ShapeDtypeStruct((3 * CELLS, samples), BF),
            jax.ShapeDtypeStruct((3 * CELLS + 16, samples), BF),
        ),
        scratch_shapes=[pltpu.VMEM((2 * CELLS, samples + weights.shape[3]), BF)],
        compiler_params=pltpu.CompilerParams(vmem_limit_bytes=16 << 20),
        name="border",
    )(place, one, other, own, weights)


TILE = 2048
WIDE = BX * CH
EDGE = 128
ALL_LINES = BI + 4
TALL = BX * CLASSES


def taps_of(padded, rows, start):
    window = padded[rows, start : start + TILE + 2 * EDGE]
    inner = slice(EDGE, EDGE + TILE)
    width = window.shape[1]
    return pltpu.roll(window, 1, 1)[:, inner], window[:, inner], pltpu.roll(window, width - 1, 1)[:, inner]


def clear_edges(padded):
    zeros = jnp.zeros((padded.shape[0], EDGE), BF)
    padded[:, :EDGE] = zeros
    padded[:, padded.shape[1] - EDGE :] = zeros


def inside(place_ref, start_x, line):
    bin_x = iota((WIDE, 1), 0) // CH + start_x + place_ref[1] * BX - 1
    bin_i = line + place_ref[0] * BI - 1
    return (bin_x >= 0) & (bin_x < place_ref[3]) & (bin_i >= 0) & (bin_i < place_ref[2])


def run_tiles(columns, first, second, keeps, split, store, volume, taps, hidden):
    samples = volume.shape[1] - 2 * EDGE
    count = len(columns)
    group = 3 * count * TALL
    clear_edges(volume)
    clear_edges(hidden)
    for which, column in enumerate(columns):
        at = 3 * which * CELLS
        volume[at : at + 3 * CELLS, EDGE : EDGE + samples] = column[: 3 * CELLS, :]

    def first_convolution(start):
        lanes = slice(start, start + TILE)
        for which in range(count):
            rows = slice(3 * which * CELLS, 3 * (which + 1) * CELLS)
            for tap, value in enumerate(taps_of(volume, rows, start)):
                for line in range(ALL_LINES):
                    at = line * group + (tap * count + which) * TALL
                    taps[at : at + TALL, lanes] = value[line * TALL : (line + 1) * TALL]
        for line in range(BI + 2):
            rows = slice(line * WIDE, (line + 1) * WIDE)
            value = split(nn(first, taps[line * group : (line + 3) * group, lanes]), rows, lanes)
            value = jnp.where(keeps[line], jax.nn.gelu(value), 0.0).astype(BF)
            hidden[rows, EDGE + start : EDGE + start + TILE] = value

    def second_convolution(start):
        held = jnp.concatenate(taps_of(hidden, slice(None), start), axis=0)
        store(nn(second, held), slice(start, start + TILE))

    for start in range(0, samples, TILE):
        first_convolution(start)
        if start:
            second_convolution(start - TILE)
    second_convolution(samples - TILE)


def near_kernel(
    place_ref, mid_ref, near_ref, first_ref, second_ref, partial_ref, sum_ref, volume, taps, hidden,
):
    start_x = jnp.where(place_ref[1] % 2 == 0, BX, 0)
    keeps = [inside(place_ref, start_x, line) for line in range(BI + 2)]

    def split(both, rows, lanes):
        partial_ref[rows, lanes] = both[WIDE:]
        return both[:WIDE]

    def store(value, lanes):
        sum_ref[:, lanes] = value

    run_tiles(
        (mid_ref, near_ref), first_ref[...], second_ref[...], keeps, split, store, volume, taps, hidden,
    )


def far_kernel(
    place_ref, far_ref, partial_ref, sum_ref, first_ref, second_ref, out_ref, volume, taps, hidden,
):
    start_x = jnp.where(place_ref[1] % 2 == 0, 0, BX)
    keeps = [inside(place_ref, start_x, line) for line in range(BI + 2)]

    def split(value, rows, lanes):
        return value + partial_ref[rows, lanes]

    def store(value, lanes):
        total = (value + sum_ref[:, lanes]).astype(BF)
        out_ref[:, :, :, lanes] = total.reshape(out_ref.shape[:3] + (TILE,))

    run_tiles(
        (far_ref,), first_ref[...], second_ref[...], keeps, split, store, volume, taps, hidden,
    )


def convolutions(place, mid, near, far, matrices):
    samples = mid.shape[1]
    first_near, first_far, second_near, second_far = matrices
    whole = pl.BlockSpec(memory_space=pltpu.VMEM)
    scalars = pl.BlockSpec(memory_space=pltpu.SMEM)
    bins = (BI + 2) * WIDE

    def buffers(count):
        return [
            pltpu.VMEM((3 * count * CELLS, samples + 2 * EDGE), BF),
            pltpu.VMEM((3 * count * ALL_LINES * TALL, samples), BF),
            pltpu.VMEM((bins, samples + 2 * EDGE), BF),
        ]

    partial, total = pl.pallas_call(
        near_kernel,
        in_specs=[scalars] + [whole] * 4,
        out_specs=(whole, whole),
        out_shape=(
            jax.ShapeDtypeStruct((bins, samples), F32),
            jax.ShapeDtypeStruct((CH * BI * BX, samples), F32),
        ),
        scratch_shapes=buffers(2),
        compiler_params=pltpu.CompilerParams(vmem_limit_bytes=24 << 20),
        cost_estimate=pl.CostEstimate(flops=0, bytes_accessed=0, transcendentals=0),
        name="near",
    )(place, mid, near, first_near, second_near)
    return pl.pallas_call(
        far_kernel,
        in_specs=[scalars] + [whole] * 5,
        out_specs=whole,
        out_shape=jax.ShapeDtypeStruct((CH, BI, BX, samples), BF),
        scratch_shapes=buffers(1),
        compiler_params=pltpu.CompilerParams(vmem_limit_bytes=24 << 20),
        name="far",
    )(place, far, partial, total, first_far, second_far)


def first_matrices(kernel, odd):
    spatial = kernel.transpose(2, 3, 4, 1, 0)
    placed = [
        jnp.pad(spatial, ((0, 0), (at, BX + 1 - at), (0, 0), (0, 0), (0, 0))) for at in range(BX + 2)
    ]
    matrix = jnp.stack(placed, axis=0).transpose(0, 5, 1, 3, 2, 4)
    mirrored = jnp.concatenate([matrix[BX:], matrix[:BX]], axis=0)
    mirrored = jnp.concatenate(
        [mirrored[..., 2 * BX :, :], mirrored[..., BX : 2 * BX, :], mirrored[..., :BX, :]], axis=4
    )
    matrix = jnp.where(odd, mirrored, matrix)
    near = jnp.concatenate([matrix[BX:, ..., BX:, :], matrix[:BX, ..., BX:, :]], axis=0)
    far = matrix[:BX, ..., :BX, :]
    return near.reshape(2 * WIDE, -1), far.reshape(WIDE, -1)


def second_matrices(kernel, odd):
    spatial = kernel.transpose(2, 3, 4, 0, 1)
    placed = [
        [
            jnp.pad(spatial, ((i, BI - 1 - i), (x, BX - 1 - x), (0, 0), (0, 0), (0, 0)))
            for x in range(BX)
        ]
        for i in range(BI)
    ]
    matrix = jnp.stack([jnp.stack(line, axis=0) for line in placed], axis=0)
    matrix = matrix.transpose(4, 5, 0, 1, 2, 3, 6)
    low, high = matrix[..., :BX, :], matrix[..., BX:, :]
    rows = CH * BI * BX
    near, far = jnp.where(odd, low, high), jnp.where(odd, high, low)
    return tuple(jnp.moveaxis(side, 0, 3).reshape(rows, -1) for side in (near, far))


def swapped(block, axis, start):
    count = lax.axis_size(axis)
    pairs = [(i, i + 1) for i in range(start, count - 1, 2)]
    return lax.ppermute(block, axis, pairs + [(j, i) for i, j in pairs])


def per_device(traces, trace_dest, trace_bin, trace_class, band_weights, conv_first, conv_second):
    inline_size = lax.axis_size("inline")
    xline_size = lax.axis_size("xline")
    devices = inline_size * xline_size
    at_i, at_x = lax.axis_index("inline"), lax.axis_index("xline")
    count, samples = traces.shape
    width = samples // 2 + 128
    outgoing = pack(
        traces,
        trace_dest.reshape(1, count),
        trace_bin.reshape(1, count),
        trace_class.reshape(1, count),
        devices,
    )
    arrived = lax.all_to_all(
        outgoing.reshape(devices, 2 * CAP, width), ALL, split_axis=0, concat_axis=0, tiled=True
    ).reshape(devices * 2 * CAP, width)
    odd_x = at_x % 2 == 1
    place = jnp.stack(
        [at_i, at_x, jnp.int32(inline_size * BI), jnp.int32(xline_size * BX)]
    ).astype(jnp.int32)
    matrices = first_matrices(conv_first, odd_x) + second_matrices(conv_second, odd_x)
    arrived, matrices, place = lax.optimization_barrier((arrived, matrices, place))
    classes, blocks, steps, band, _ = band_weights.shape
    weights = band_weights.reshape(classes, blocks, steps * band, band)
    averaged = stack(arrived)
    one, other = swapped(averaged, "inline", 0), swapped(averaged, "inline", 1)
    volume, weights = moved_out(averaged, weights)
    column, sent = border(place, one, other, volume, weights)
    far = swapped(sent, "xline", 1)
    near = swapped(column, "xline", 0)
    return convolutions(place, column, near, far, matrices)


def solution(mesh):
    return jax.shard_map(
        per_device,
        mesh=mesh,
        in_specs=(
            P(ALL, None),
            P(ALL, None),
            P(ALL),
            P(ALL),
            P(),
            P(),
            P(),
        ),
        out_specs=P(None, "inline", "xline", None),
        check_vma=False,
    )
```

```python
import jax
import jax.numpy as jnp
import numpy as np
from jax import lax
from jax.experimental import pallas as pl
from jax.experimental.pallas import tpu as pltpu
from jax.sharding import PartitionSpec as P

CLASSES = 8
BI = 2
BX = 2
CH = 32
CAP = 4
ALL = ("inline", "xline")
BF = jnp.bfloat16
F32 = jnp.float32
CELLS = CLASSES * BI * BX


def iota(shape, dim):
    return lax.broadcasted_iota(jnp.int32, shape, dim)


def nt(a, b):
    return lax.dot_general(a, b, (((1,), (1,)), ((), ())), preferred_element_type=F32)


def tn(a, b):
    return lax.dot_general(a, b, (((0,), (0,)), ((), ())), preferred_element_type=F32)


def nn(a, b):
    return jnp.dot(a, b, preferred_element_type=F32)


def before(count):
    return (iota((count, count), 0) < iota((count, count), 1)).astype(BF)


def pack_kernel(
    dest_ref, bin_ref, class_ref, traces_ref, out_ref, tags, loaded, packed, tag_sem, load_sem, store_sem
):
    rows, width = packed.shape
    count, half = loaded.shape[0] // 2, loaded.shape[1]
    devices = rows // (2 * CAP)
    parts = store_sem.shape[0]
    each = rows // parts
    small = []
    for number, ref in enumerate((dest_ref, bin_ref, class_ref)):
        small.append(pltpu.make_async_copy(ref, tags.at[number], tag_sem.at[number]))
        small[-1].start()
    loads = []
    for side in range(2):
        loads.append(
            pltpu.make_async_copy(
                traces_ref.at[:, pl.ds(side * half, half)],
                loaded.at[pl.ds(side * count, count)],
                load_sem.at[side],
            )
        )
        loads[-1].start()
    for copy in small:
        copy.wait()
    dest = tags[0]
    named = iota((devices, count), 0) == dest
    rank = nn(named.astype(BF), before(count))
    slot = jnp.sum(jnp.where(named, rank, 0.0), axis=0, keepdims=True)
    position = dest * (2 * CAP) + slot.astype(jnp.int32)
    cell = tags[1] * CLASSES + tags[2]
    lane = iota((128, count), 0)
    tagged = jnp.concatenate(
        [((lane == cell) | (lane == 127)).astype(BF), (lane == cell + CELLS).astype(BF)], axis=1
    )
    for load in loads:
        load.wait()
    stores = []
    for part in range(parts):
        piece = slice(part * each, (part + 1) * each)
        row = iota((each, count), 0) + part * each
        place = jnp.concatenate(
            [(row == position).astype(BF), (row == position + CAP).astype(BF)], axis=1
        )
        packed[piece, half:] = nt(place, tagged).astype(BF)
        packed[piece, :half] = nn(place, loaded[...]).astype(BF)
        chunk = pl.ds(part * each, each)
        stores.append(pltpu.make_async_copy(packed.at[chunk], out_ref.at[chunk], store_sem.at[part]))
        stores[-1].start()
    for copy in stores:
        copy.wait()


def pack(traces, dest, bins, classes, devices):
    count, samples = traces.shape
    rows, width = devices * 2 * CAP, samples // 2 + 128
    kept = pl.BlockSpec(memory_space=pltpu.HBM)
    pin = lambda array: pltpu.with_memory_space_constraint(array, pltpu.HBM)
    return pl.pallas_call(
        pack_kernel,
        in_specs=[kept] * 4,
        out_specs=kept,
        out_shape=pltpu.HBM((rows, width), BF),
        scratch_shapes=[
            pltpu.VMEM((3, 1, count), jnp.int32),
            pltpu.VMEM((2 * count, samples // 2), BF),
            pltpu.VMEM((rows, width), BF),
            pltpu.SemaphoreType.DMA((3,)),
            pltpu.SemaphoreType.DMA((2,)),
            pltpu.SemaphoreType.DMA((4,)),
        ],
        compiler_params=pltpu.CompilerParams(vmem_limit_bytes=24 << 20),
        name="pack",
    )(pin(dest), pin(bins), pin(classes), pin(traces))


def stack_kernel(arrived_ref, out_ref):
    width = arrived_ref.shape[1]
    half = width - 128
    stacked = tn(arrived_ref[:, half:], arrived_ref[...])
    fold = jnp.maximum(stacked[:CELLS, width - 1 : width], 1.0)
    out_ref[:, :half] = (stacked[:CELLS, :half] / fold).astype(BF)
    out_ref[:, half:] = (stacked[CELLS : 2 * CELLS, :half] / fold).astype(BF)


def stack(arrived):
    rows, width = arrived.shape
    whole = pl.BlockSpec(memory_space=pltpu.VMEM)
    return pl.pallas_call(
        stack_kernel,
        in_specs=[whole],
        out_specs=whole,
        out_shape=jax.ShapeDtypeStruct((CELLS, 2 * (width - 128)), BF),
        compiler_params=pltpu.CompilerParams(vmem_limit_bytes=12 << 20),
        name="stack",
    )(arrived)


def band_loads(source_ref, weights, sem, sizes):
    loads, first = {}, 0
    for number, size in enumerate(sizes):
        blocks = pl.ds(first, size)
        loads[first] = pltpu.make_async_copy(source_ref.at[:, blocks], weights.at[:, blocks], sem.at[number])
        loads[first].start()
        first += size
    return loads


def moved_block(averaged, weights, block, loads):
    if block in loads:
        loads[block].wait()
    classes, _, _, band = weights.shape
    start = block * band
    wide = jnp.concatenate([weights[number, block] for number in range(classes)], axis=1)
    moved = nn(averaged[:, start : start + 2 * band], wide)
    kind = iota((averaged.shape[0], band), 0) % classes
    total = moved[:, :band]
    for number in range(1, classes):
        total = jnp.where(kind == number, moved[:, number * band : (number + 1) * band], total)
    return total.astype(BF)


BAND_SIZES = (2, 2, 2, 2, 2, 2, 2, 2)


def band_kernel(averaged_ref, band_ref, out_ref, weights, padded, sem):
    loads = band_loads(band_ref, weights, sem, BAND_SIZES)
    rows, samples = averaged_ref.shape
    band = weights.shape[3]
    padded[:, :samples] = averaged_ref[...]
    padded[:, samples:] = jnp.zeros((rows, band), BF)
    for block in range(weights.shape[1]):
        out_ref[:, block * band : (block + 1) * band] = moved_block(padded, weights, block, loads)


def moved_out(averaged, weights):
    rows, samples = averaged.shape
    whole = pl.BlockSpec(memory_space=pltpu.VMEM)
    return pl.pallas_call(
        band_kernel,
        in_specs=[whole, pl.BlockSpec(memory_space=pltpu.HBM)],
        out_specs=(whole, whole),
        out_shape=(jax.ShapeDtypeStruct((rows, samples), BF), jax.ShapeDtypeStruct(weights.shape, BF)),
        scratch_shapes=[
            pltpu.VMEM((rows, samples + weights.shape[3]), BF),
            pltpu.SemaphoreType.DMA((len(BAND_SIZES),)),
        ],
        compiler_params=pltpu.CompilerParams(vmem_limit_bytes=16 << 20),
        name="band",
    )(averaged, pltpu.with_memory_space_constraint(weights, pltpu.HBM))


def border_kernel(
    place_ref, one_ref, other_ref, own_ref, weights, column_ref, top_ref, bottom_ref, padded
):
    samples = own_ref.shape[1]
    band = weights.shape[3]
    odd = place_ref[0] % 2 == 1
    one, other = one_ref[...], other_ref[...]
    padded[:CELLS, :samples] = jnp.where(odd, one, other)
    padded[CELLS:, :samples] = jnp.where(odd, other, one)
    padded[:, samples:] = jnp.zeros((2 * CELLS, band), BF)
    own = own_ref[...]
    column_ref[CELLS : 2 * CELLS, :] = own
    top_ref[CELLS:, :] = own[: CELLS // 2]
    bottom_ref[: CELLS // 2, :] = own[CELLS // 2 :]
    for block in range(weights.shape[1]):
        lanes = slice(block * band, (block + 1) * band)
        total = moved_block(padded, weights, block, {})
        column_ref[:CELLS, lanes] = total[:CELLS]
        column_ref[2 * CELLS :, lanes] = total[CELLS:]
        top_ref[:CELLS, lanes] = total[:CELLS]
        bottom_ref[CELLS // 2 :, lanes] = total[CELLS:]


def border(place, one, other, own, weights):
    samples = own.shape[1]
    whole = pl.BlockSpec(memory_space=pltpu.VMEM)
    return pl.pallas_call(
        border_kernel,
        in_specs=[pl.BlockSpec(memory_space=pltpu.SMEM)] + [whole] * 4,
        out_specs=(whole, whole, whole),
        out_shape=(
            jax.ShapeDtypeStruct((3 * CELLS, samples), BF),
            jax.ShapeDtypeStruct((3 * CELLS // 2, samples), BF),
            jax.ShapeDtypeStruct((3 * CELLS // 2, samples), BF),
        ),
        scratch_shapes=[pltpu.VMEM((2 * CELLS, samples + weights.shape[3]), BF)],
        compiler_params=pltpu.CompilerParams(vmem_limit_bytes=16 << 20),
        name="border",
    )(place, one, other, own, weights)


TILE = 2048
WIDE = BX * CH
EDGE = 128
ALL_LINES = BI + 4
TALL = BX * CLASSES


def taps_of(padded, rows, start):
    window = padded[rows, start : start + TILE + 2 * EDGE]
    inner = slice(EDGE, EDGE + TILE)
    width = window.shape[1]
    return pltpu.roll(window, 1, 1)[:, inner], window[:, inner], pltpu.roll(window, width - 1, 1)[:, inner]


def clear_edges(padded):
    zeros = jnp.zeros((padded.shape[0], EDGE), BF)
    padded[:, :EDGE] = zeros
    padded[:, padded.shape[1] - EDGE :] = zeros


def inside(place_ref, start_x, line):
    bin_x = iota((WIDE, 1), 0) // CH + start_x + place_ref[1] * BX - 1
    bin_i = line + place_ref[0] * BI - 1
    return (bin_x >= 0) & (bin_x < place_ref[3]) & (bin_i >= 0) & (bin_i < place_ref[2])


def run_tiles(columns, first, second, keeps, split, store, volume, taps, hidden):
    samples = volume.shape[1] - 2 * EDGE
    count = len(columns)
    group = 3 * count * TALL
    clear_edges(volume)
    clear_edges(hidden)
    for which, column in enumerate(columns):
        at = 3 * which * CELLS
        for piece in column:
            volume[at : at + piece.shape[0], EDGE : EDGE + samples] = piece[...]
            at += piece.shape[0]

    def first_convolution(start):
        lanes = slice(start, start + TILE)
        for which in range(count):
            rows = slice(3 * which * CELLS, 3 * (which + 1) * CELLS)
            for tap, value in enumerate(taps_of(volume, rows, start)):
                for line in range(ALL_LINES):
                    at = line * group + (tap * count + which) * TALL
                    taps[at : at + TALL, lanes] = value[line * TALL : (line + 1) * TALL]
        for line in range(BI + 2):
            rows = slice(line * WIDE, (line + 1) * WIDE)
            value = split(nn(first, taps[line * group : (line + 3) * group, lanes]), rows, lanes)
            value = jnp.where(keeps[line], jax.nn.gelu(value), 0.0).astype(BF)
            hidden[rows, EDGE + start : EDGE + start + TILE] = value

    def second_convolution(start):
        held = jnp.concatenate(taps_of(hidden, slice(None), start), axis=0)
        store(nn(second, held), slice(start, start + TILE))

    for start in range(0, samples, TILE):
        first_convolution(start)
        if start:
            second_convolution(start - TILE)
    second_convolution(samples - TILE)


def near_kernel(
    place_ref, mid_ref, top_ref, bottom_ref, first_ref, second_ref,
    partial_ref, sum_ref, volume, taps, hidden,
):
    start_x = jnp.where(place_ref[1] % 2 == 0, BX, 0)
    keeps = [inside(place_ref, start_x, line) for line in range(BI + 2)]

    def split(both, rows, lanes):
        partial_ref[rows, lanes] = both[WIDE:]
        return both[:WIDE]

    def store(value, lanes):
        sum_ref[:, lanes] = value

    run_tiles(
        ((mid_ref,), (top_ref, bottom_ref)), first_ref[...], second_ref[...], keeps, split, store,
        volume, taps, hidden,
    )


def far_kernel(
    place_ref, far_ref, partial_ref, sum_ref, first_ref, second_ref, out_ref, volume, taps, hidden,
):
    start_x = jnp.where(place_ref[1] % 2 == 0, 0, BX)
    keeps = [inside(place_ref, start_x, line) for line in range(BI + 2)]

    def split(value, rows, lanes):
        return value + partial_ref[rows, lanes]

    def store(value, lanes):
        total = (value + sum_ref[:, lanes]).astype(BF)
        out_ref[:, :, :, lanes] = total.reshape(out_ref.shape[:3] + (TILE,))

    run_tiles(
        ((far_ref,),), first_ref[...], second_ref[...], keeps, split, store, volume, taps, hidden,
    )


def convolutions(place, mid, top, bottom, far, matrices):
    samples = mid.shape[1]
    first_near, first_far, second_near, second_far = matrices
    whole = pl.BlockSpec(memory_space=pltpu.VMEM)
    scalars = pl.BlockSpec(memory_space=pltpu.SMEM)
    bins = (BI + 2) * WIDE

    def buffers(count):
        return [
            pltpu.VMEM((3 * count * CELLS, samples + 2 * EDGE), BF),
            pltpu.VMEM((3 * count * ALL_LINES * TALL, samples), BF),
            pltpu.VMEM((bins, samples + 2 * EDGE), BF),
        ]

    partial, total = pl.pallas_call(
        near_kernel,
        in_specs=[scalars] + [whole] * 5,
        out_specs=(whole, whole),
        out_shape=(
            jax.ShapeDtypeStruct((bins, samples), F32),
            jax.ShapeDtypeStruct((CH * BI * BX, samples), F32),
        ),
        scratch_shapes=buffers(2),
        compiler_params=pltpu.CompilerParams(vmem_limit_bytes=24 << 20),
        cost_estimate=pl.CostEstimate(flops=0, bytes_accessed=0, transcendentals=0),
        name="near",
    )(place, mid, top, bottom, first_near, second_near)
    return pl.pallas_call(
        far_kernel,
        in_specs=[scalars] + [whole] * 5,
        out_specs=whole,
        out_shape=jax.ShapeDtypeStruct((CH, BI, BX, samples), BF),
        scratch_shapes=buffers(1),
        compiler_params=pltpu.CompilerParams(vmem_limit_bytes=24 << 20),
        name="far",
    )(place, far, partial, total, first_far, second_far)


def first_matrices(kernel, odd):
    spatial = kernel.transpose(2, 3, 4, 1, 0)
    placed = [
        jnp.pad(spatial, ((0, 0), (at, BX + 1 - at), (0, 0), (0, 0), (0, 0))) for at in range(BX + 2)
    ]
    matrix = jnp.stack(placed, axis=0).transpose(0, 5, 1, 3, 2, 4)
    mirrored = jnp.concatenate([matrix[BX:], matrix[:BX]], axis=0)
    mirrored = jnp.concatenate(
        [mirrored[..., 2 * BX :, :], mirrored[..., BX : 2 * BX, :], mirrored[..., :BX, :]], axis=4
    )
    matrix = jnp.where(odd, mirrored, matrix)
    near = jnp.concatenate([matrix[BX:, ..., BX:, :], matrix[:BX, ..., BX:, :]], axis=0)
    far = matrix[:BX, ..., :BX, :]
    return near.reshape(2 * WIDE, -1), far.reshape(WIDE, -1)


def second_matrices(kernel, odd):
    spatial = kernel.transpose(2, 3, 4, 0, 1)
    placed = [
        [
            jnp.pad(spatial, ((i, BI - 1 - i), (x, BX - 1 - x), (0, 0), (0, 0), (0, 0)))
            for x in range(BX)
        ]
        for i in range(BI)
    ]
    matrix = jnp.stack([jnp.stack(line, axis=0) for line in placed], axis=0)
    matrix = matrix.transpose(4, 5, 0, 1, 2, 3, 6)
    low, high = matrix[..., :BX, :], matrix[..., BX:, :]
    rows = CH * BI * BX
    near, far = jnp.where(odd, low, high), jnp.where(odd, high, low)
    return tuple(jnp.moveaxis(side, 0, 3).reshape(rows, -1) for side in (near, far))


def swapped(block, axis, start):
    count = lax.axis_size(axis)
    pairs = [(i, i + 1) for i in range(start, count - 1, 2)]
    return lax.ppermute(block, axis, pairs + [(j, i) for i, j in pairs])


def per_device(traces, trace_dest, trace_bin, trace_class, band_weights, conv_first, conv_second):
    inline_size = lax.axis_size("inline")
    xline_size = lax.axis_size("xline")
    devices = inline_size * xline_size
    at_i, at_x = lax.axis_index("inline"), lax.axis_index("xline")
    count, samples = traces.shape
    width = samples // 2 + 128
    outgoing = pack(
        traces,
        trace_dest.reshape(1, count),
        trace_bin.reshape(1, count),
        trace_class.reshape(1, count),
        devices,
    )
    arrived = lax.all_to_all(
        outgoing.reshape(devices, 2 * CAP, width), ALL, split_axis=0, concat_axis=0, tiled=True
    ).reshape(devices * 2 * CAP, width)
    odd_x = at_x % 2 == 1
    place = jnp.stack(
        [at_i, at_x, jnp.int32(inline_size * BI), jnp.int32(xline_size * BX)]
    ).astype(jnp.int32)
    matrices = first_matrices(conv_first, odd_x) + second_matrices(conv_second, odd_x)
    arrived, matrices, place = lax.optimization_barrier((arrived, matrices, place))
    classes, blocks, steps, band, _ = band_weights.shape
    weights = band_weights.reshape(classes, blocks, steps * band, band)
    averaged = stack(arrived)
    one, other = swapped(averaged, "inline", 0), swapped(averaged, "inline", 1)
    volume, weights = moved_out(averaged, weights)
    column, top, bottom = border(place, one, other, volume, weights)
    far = swapped(column, "xline", 1)
    top, bottom = swapped(top, "xline", 0), swapped(bottom, "xline", 0)
    return convolutions(place, column, top, bottom, far, matrices)


def solution(mesh):
    return jax.shard_map(
        per_device,
        mesh=mesh,
        in_specs=(
            P(ALL, None),
            P(ALL, None),
            P(ALL),
            P(ALL),
            P(),
            P(),
            P(),
        ),
        out_specs=P(None, "inline", "xline", None),
        check_vma=False,
    )
```

```python
import jax
import jax.numpy as jnp
import numpy as np
from jax import lax
from jax.experimental import pallas as pl
from jax.experimental.pallas import tpu as pltpu
from jax.sharding import PartitionSpec as P

CLASSES = 8
BI = 2
BX = 2
CH = 32
CAP = 4
ALL = ("inline", "xline")
BF = jnp.bfloat16
F32 = jnp.float32
CELLS = CLASSES * BI * BX


def iota(shape, dim):
    return lax.broadcasted_iota(jnp.int32, shape, dim)


def nt(a, b):
    return lax.dot_general(a, b, (((1,), (1,)), ((), ())), preferred_element_type=F32)


def tn(a, b):
    return lax.dot_general(a, b, (((0,), (0,)), ((), ())), preferred_element_type=F32)


def nn(a, b):
    return jnp.dot(a, b, preferred_element_type=F32)


def before(count):
    return (iota((count, count), 0) < iota((count, count), 1)).astype(BF)


def pack_kernel(
    dest_ref, bin_ref, class_ref, traces_ref, out_ref, tags, loaded, packed, tag_sem, load_sem, store_sem
):
    rows, width = packed.shape
    count, half = loaded.shape[0] // 2, loaded.shape[1]
    devices = rows // (2 * CAP)
    parts = store_sem.shape[0]
    each = rows // parts
    small = []
    for number, ref in enumerate((dest_ref, bin_ref, class_ref)):
        small.append(pltpu.make_async_copy(ref, tags.at[number], tag_sem.at[number]))
        small[-1].start()
    loads = []
    for side in range(2):
        loads.append(
            pltpu.make_async_copy(
                traces_ref.at[:, pl.ds(side * half, half)],
                loaded.at[pl.ds(side * count, count)],
                load_sem.at[side],
            )
        )
        loads[-1].start()
    for copy in small:
        copy.wait()
    dest = tags[0]
    named = iota((devices, count), 0) == dest
    rank = nn(named.astype(BF), before(count))
    slot = jnp.sum(jnp.where(named, rank, 0.0), axis=0, keepdims=True)
    position = dest * (2 * CAP) + slot.astype(jnp.int32)
    cell = tags[1] * CLASSES + tags[2]
    lane = iota((128, count), 0)
    tagged = jnp.concatenate(
        [((lane == cell) | (lane == 127)).astype(BF), (lane == cell + CELLS).astype(BF)], axis=1
    )
    for load in loads:
        load.wait()
    stores = []
    for part in range(parts):
        piece = slice(part * each, (part + 1) * each)
        row = iota((each, count), 0) + part * each
        place = jnp.concatenate(
            [(row == position).astype(BF), (row == position + CAP).astype(BF)], axis=1
        )
        packed[piece, half:] = nt(place, tagged).astype(BF)
        packed[piece, :half] = nn(place, loaded[...]).astype(BF)
        chunk = pl.ds(part * each, each)
        stores.append(pltpu.make_async_copy(packed.at[chunk], out_ref.at[chunk], store_sem.at[part]))
        stores[-1].start()
    for copy in stores:
        copy.wait()


def pack(traces, dest, bins, classes, devices):
    count, samples = traces.shape
    rows, width = devices * 2 * CAP, samples // 2 + 128
    kept = pl.BlockSpec(memory_space=pltpu.HBM)
    pin = lambda array: pltpu.with_memory_space_constraint(array, pltpu.HBM)
    return pl.pallas_call(
        pack_kernel,
        in_specs=[kept] * 4,
        out_specs=kept,
        out_shape=pltpu.HBM((rows, width), BF),
        scratch_shapes=[
            pltpu.VMEM((3, 1, count), jnp.int32),
            pltpu.VMEM((2 * count, samples // 2), BF),
            pltpu.VMEM((rows, width), BF),
            pltpu.SemaphoreType.DMA((3,)),
            pltpu.SemaphoreType.DMA((2,)),
            pltpu.SemaphoreType.DMA((4,)),
        ],
        compiler_params=pltpu.CompilerParams(vmem_limit_bytes=24 << 20),
        name="pack",
    )(pin(dest), pin(bins), pin(classes), pin(traces))


def stack_kernel(arrived_ref, out_ref):
    width = arrived_ref.shape[1]
    half = width - 128
    stacked = tn(arrived_ref[:, half:], arrived_ref[...])
    fold = jnp.maximum(stacked[:CELLS, width - 1 : width], 1.0)
    out_ref[:, :half] = (stacked[:CELLS, :half] / fold).astype(BF)
    out_ref[:, half:] = (stacked[CELLS : 2 * CELLS, :half] / fold).astype(BF)


def stack(arrived):
    rows, width = arrived.shape
    whole = pl.BlockSpec(memory_space=pltpu.VMEM)
    return pl.pallas_call(
        stack_kernel,
        in_specs=[whole],
        out_specs=whole,
        out_shape=jax.ShapeDtypeStruct((CELLS, 2 * (width - 128)), BF),
        compiler_params=pltpu.CompilerParams(vmem_limit_bytes=12 << 20),
        name="stack",
    )(arrived)


def band_loads(source_ref, weights, sem, sizes):
    loads, first = {}, 0
    for number, size in enumerate(sizes):
        blocks = pl.ds(first, size)
        loads[first] = pltpu.make_async_copy(source_ref.at[:, blocks], weights.at[:, blocks], sem.at[number])
        loads[first].start()
        first += size
    return loads


def moved_block(averaged, weights, block, loads):
    if block in loads:
        loads[block].wait()
    classes, _, _, band = weights.shape
    start = block * band
    wide = jnp.concatenate([weights[number, block] for number in range(classes)], axis=1)
    moved = nn(averaged[:, start : start + 2 * band], wide)
    kind = iota((averaged.shape[0], band), 0) % classes
    total = moved[:, :band]
    for number in range(1, classes):
        total = jnp.where(kind == number, moved[:, number * band : (number + 1) * band], total)
    return total.astype(BF)


BAND_SIZES = (2, 2, 2, 2, 2, 2, 2, 2)


def band_kernel(averaged_ref, band_ref, out_ref, weights, padded, sem):
    loads = band_loads(band_ref, weights, sem, BAND_SIZES)
    rows, samples = averaged_ref.shape
    band = weights.shape[3]
    padded[:, :samples] = averaged_ref[...]
    padded[:, samples:] = jnp.zeros((rows, band), BF)
    for block in range(weights.shape[1]):
        out_ref[:, block * band : (block + 1) * band] = moved_block(padded, weights, block, loads)


def moved_out(averaged, weights):
    rows, samples = averaged.shape
    whole = pl.BlockSpec(memory_space=pltpu.VMEM)
    return pl.pallas_call(
        band_kernel,
        in_specs=[whole, pl.BlockSpec(memory_space=pltpu.HBM)],
        out_specs=(whole, whole),
        out_shape=(jax.ShapeDtypeStruct((rows, samples), BF), jax.ShapeDtypeStruct(weights.shape, BF)),
        scratch_shapes=[
            pltpu.VMEM((rows, samples + weights.shape[3]), BF),
            pltpu.SemaphoreType.DMA((len(BAND_SIZES),)),
        ],
        compiler_params=pltpu.CompilerParams(vmem_limit_bytes=16 << 20),
        name="band",
    )(averaged, pltpu.with_memory_space_constraint(weights, pltpu.HBM))


def border_kernel(
    place_ref, one_ref, other_ref, own_ref, weights, column_ref, top_ref, bottom_ref, padded
):
    samples = own_ref.shape[1]
    band = weights.shape[3]
    odd = place_ref[0] % 2 == 1
    one, other = one_ref[...], other_ref[...]
    padded[:CELLS, :samples] = jnp.where(odd, one, other)
    padded[CELLS:, :samples] = jnp.where(odd, other, one)
    padded[:, samples:] = jnp.zeros((2 * CELLS, band), BF)
    own = own_ref[...]
    column_ref[CELLS : 2 * CELLS, :] = own
    top_ref[CELLS:, :] = own[: CELLS // 2]
    bottom_ref[: CELLS // 2, :] = own[CELLS // 2 :]
    for block in range(weights.shape[1]):
        lanes = slice(block * band, (block + 1) * band)
        total = moved_block(padded, weights, block, {})
        column_ref[:CELLS, lanes] = total[:CELLS]
        column_ref[2 * CELLS :, lanes] = total[CELLS:]
        top_ref[:CELLS, lanes] = total[:CELLS]
        bottom_ref[CELLS // 2 :, lanes] = total[CELLS:]


def border(place, one, other, own, weights):
    samples = own.shape[1]
    whole = pl.BlockSpec(memory_space=pltpu.VMEM)
    return pl.pallas_call(
        border_kernel,
        in_specs=[pl.BlockSpec(memory_space=pltpu.SMEM)] + [whole] * 4,
        out_specs=(whole, whole, whole),
        out_shape=(
            jax.ShapeDtypeStruct((3 * CELLS, samples), BF),
            jax.ShapeDtypeStruct((3 * CELLS // 2, samples), BF),
            jax.ShapeDtypeStruct((3 * CELLS // 2, samples), BF),
        ),
        scratch_shapes=[pltpu.VMEM((2 * CELLS, samples + weights.shape[3]), BF)],
        compiler_params=pltpu.CompilerParams(vmem_limit_bytes=16 << 20),
        name="border",
    )(place, one, other, own, weights)


TILE = 2048
PART = 1024
WIDE = BX * CH
EDGE = 128
ALL_LINES = BI + 4
TALL = BX * CLASSES


def taps_of(padded, rows, start, size):
    window = padded[rows, start : start + size + 2 * EDGE]
    inner = slice(EDGE, EDGE + size)
    width = window.shape[1]
    return pltpu.roll(window, 1, 1)[:, inner], window[:, inner], pltpu.roll(window, width - 1, 1)[:, inner]


def clear_edges(padded):
    zeros = jnp.zeros((padded.shape[0], EDGE), BF)
    padded[:, :EDGE] = zeros
    padded[:, padded.shape[1] - EDGE :] = zeros


def inside(place_ref, start_x, line):
    bin_x = iota((WIDE, 1), 0) // CH + start_x + place_ref[1] * BX - 1
    bin_i = line + place_ref[0] * BI - 1
    return (bin_x >= 0) & (bin_x < place_ref[3]) & (bin_i >= 0) & (bin_i < place_ref[2])


def run_tiles(columns, first, second, keeps, split, store, volume, taps, hidden):
    samples = volume.shape[1] - 2 * EDGE
    count = len(columns)
    group = 3 * count * TALL
    clear_edges(volume)
    clear_edges(hidden)
    for which, column in enumerate(columns):
        at = 3 * which * CELLS
        for piece in column:
            volume[at : at + piece.shape[0], EDGE : EDGE + samples] = piece[...]
            at += piece.shape[0]

    def first_convolution(start):
        lanes = slice(start, start + TILE)
        for which in range(count):
            rows = slice(3 * which * CELLS, 3 * (which + 1) * CELLS)
            for tap, value in enumerate(taps_of(volume, rows, start, TILE)):
                for line in range(ALL_LINES):
                    at = line * group + (tap * count + which) * TALL
                    taps[at : at + TALL, lanes] = value[line * TALL : (line + 1) * TALL]
        for line in range(BI + 2):
            rows = slice(line * WIDE, (line + 1) * WIDE)
            value = split(nn(first, taps[line * group : (line + 3) * group, lanes]), rows, lanes)
            value = jnp.where(keeps[line], jax.nn.gelu(value), 0.0).astype(BF)
            hidden[rows, EDGE + start : EDGE + start + TILE] = value

    def second_convolution(start):
        for at in range(start, start + TILE, PART):
            held = jnp.concatenate(taps_of(hidden, slice(None), at, PART), axis=0)
            store(nn(second, held), slice(at, at + PART))

    for start in range(0, samples, TILE):
        first_convolution(start)
        if start:
            second_convolution(start - TILE)
    second_convolution(samples - TILE)


def near_kernel(
    place_ref, mid_ref, top_ref, bottom_ref, first_ref, second_ref,
    partial_ref, sum_ref, volume, taps, hidden,
):
    start_x = jnp.where(place_ref[1] % 2 == 0, BX, 0)
    keeps = [inside(place_ref, start_x, line) for line in range(BI + 2)]

    def split(both, rows, lanes):
        partial_ref[rows, lanes] = both[WIDE:]
        return both[:WIDE]

    def store(value, lanes):
        sum_ref[:, lanes] = value

    run_tiles(
        ((mid_ref,), (top_ref, bottom_ref)), first_ref[...], second_ref[...], keeps, split, store,
        volume, taps, hidden,
    )


def far_kernel(
    place_ref, far_ref, partial_ref, sum_ref, first_ref, second_ref, out_ref, volume, taps, hidden, made, sem,
):
    copies = []
    start_x = jnp.where(place_ref[1] % 2 == 0, 0, BX)
    keeps = [inside(place_ref, start_x, line) for line in range(BI + 2)]

    def split(value, rows, lanes):
        return value + partial_ref[rows, lanes]

    def store(value, lanes):
        total = (value + sum_ref[:, lanes]).astype(BF)
        number = lanes.start // PART
        made[number] = total.reshape(made.shape[1:])
        copies.append(
            pltpu.make_async_copy(made.at[number], out_ref.at[:, :, :, pl.ds(lanes.start, PART)], sem.at[number])
        )
        copies[-1].start()

    run_tiles(
        ((far_ref,),), first_ref[...], second_ref[...], keeps, split, store, volume, taps, hidden,
    )
    for copy in copies:
        copy.wait()


def convolutions(place, mid, top, bottom, far, matrices):
    samples = mid.shape[1]
    first_near, first_far, second_near, second_far = matrices
    whole = pl.BlockSpec(memory_space=pltpu.VMEM)
    scalars = pl.BlockSpec(memory_space=pltpu.SMEM)
    bins = (BI + 2) * WIDE

    def buffers(count):
        return [
            pltpu.VMEM((3 * count * CELLS, samples + 2 * EDGE), BF),
            pltpu.VMEM((3 * count * ALL_LINES * TALL, samples), BF),
            pltpu.VMEM((bins, samples + 2 * EDGE), BF),
        ]

    partial, total = pl.pallas_call(
        near_kernel,
        in_specs=[scalars] + [whole] * 5,
        out_specs=(whole, whole),
        out_shape=(
            jax.ShapeDtypeStruct((bins, samples), F32),
            jax.ShapeDtypeStruct((CH * BI * BX, samples), F32),
        ),
        scratch_shapes=buffers(2),
        compiler_params=pltpu.CompilerParams(vmem_limit_bytes=24 << 20),
        cost_estimate=pl.CostEstimate(flops=0, bytes_accessed=0, transcendentals=0),
        name="near",
    )(place, mid, top, bottom, first_near, second_near)
    return pl.pallas_call(
        far_kernel,
        in_specs=[scalars] + [whole] * 5,
        out_specs=pl.BlockSpec(memory_space=pltpu.HBM),
        out_shape=pltpu.HBM((CH, BI, BX, samples), BF),
        scratch_shapes=buffers(1)
        + [
            pltpu.VMEM((samples // PART, CH, BI, BX, PART), BF),
            pltpu.SemaphoreType.DMA((samples // PART,)),
        ],
        compiler_params=pltpu.CompilerParams(vmem_limit_bytes=24 << 20),
        name="far",
    )(place, far, partial, total, first_far, second_far)


def first_matrices(kernel, odd):
    spatial = kernel.transpose(2, 3, 4, 1, 0)
    placed = [
        jnp.pad(spatial, ((0, 0), (at, BX + 1 - at), (0, 0), (0, 0), (0, 0))) for at in range(BX + 2)
    ]
    matrix = jnp.stack(placed, axis=0).transpose(0, 5, 1, 3, 2, 4)
    mirrored = jnp.concatenate([matrix[BX:], matrix[:BX]], axis=0)
    mirrored = jnp.concatenate(
        [mirrored[..., 2 * BX :, :], mirrored[..., BX : 2 * BX, :], mirrored[..., :BX, :]], axis=4
    )
    matrix = jnp.where(odd, mirrored, matrix)
    near = jnp.concatenate([matrix[BX:, ..., BX:, :], matrix[:BX, ..., BX:, :]], axis=0)
    far = matrix[:BX, ..., :BX, :]
    return near.reshape(2 * WIDE, -1), far.reshape(WIDE, -1)


def second_matrices(kernel, odd):
    spatial = kernel.transpose(2, 3, 4, 0, 1)
    placed = [
        [
            jnp.pad(spatial, ((i, BI - 1 - i), (x, BX - 1 - x), (0, 0), (0, 0), (0, 0)))
            for x in range(BX)
        ]
        for i in range(BI)
    ]
    matrix = jnp.stack([jnp.stack(line, axis=0) for line in placed], axis=0)
    matrix = matrix.transpose(4, 5, 0, 1, 2, 3, 6)
    low, high = matrix[..., :BX, :], matrix[..., BX:, :]
    rows = CH * BI * BX
    near, far = jnp.where(odd, low, high), jnp.where(odd, high, low)
    return tuple(jnp.moveaxis(side, 0, 3).reshape(rows, -1) for side in (near, far))


def swapped(block, axis, start):
    count = lax.axis_size(axis)
    pairs = [(i, i + 1) for i in range(start, count - 1, 2)]
    return lax.ppermute(block, axis, pairs + [(j, i) for i, j in pairs])


def per_device(traces, trace_dest, trace_bin, trace_class, band_weights, conv_first, conv_second):
    inline_size = lax.axis_size("inline")
    xline_size = lax.axis_size("xline")
    devices = inline_size * xline_size
    at_i, at_x = lax.axis_index("inline"), lax.axis_index("xline")
    count, samples = traces.shape
    width = samples // 2 + 128
    outgoing = pack(
        traces,
        trace_dest.reshape(1, count),
        trace_bin.reshape(1, count),
        trace_class.reshape(1, count),
        devices,
    )
    arrived = lax.all_to_all(
        outgoing.reshape(devices, 2 * CAP, width), ALL, split_axis=0, concat_axis=0, tiled=True
    ).reshape(devices * 2 * CAP, width)
    odd_x = at_x % 2 == 1
    place = jnp.stack(
        [at_i, at_x, jnp.int32(inline_size * BI), jnp.int32(xline_size * BX)]
    ).astype(jnp.int32)
    matrices = first_matrices(conv_first, odd_x) + second_matrices(conv_second, odd_x)
    arrived, matrices, place = lax.optimization_barrier((arrived, matrices, place))
    classes, blocks, steps, band, _ = band_weights.shape
    weights = band_weights.reshape(classes, blocks, steps * band, band)
    averaged = stack(arrived)
    one, other = swapped(averaged, "inline", 0), swapped(averaged, "inline", 1)
    volume, weights = moved_out(averaged, weights)
    column, top, bottom = border(place, one, other, volume, weights)
    far = swapped(column, "xline", 1)
    top, bottom = swapped(top, "xline", 0), swapped(bottom, "xline", 0)
    return convolutions(place, column, top, bottom, far, matrices)


def solution(mesh):
    return jax.shard_map(
        per_device,
        mesh=mesh,
        in_specs=(
            P(ALL, None),
            P(ALL, None),
            P(ALL),
            P(ALL),
            P(),
            P(),
            P(),
        ),
        out_specs=P(None, "inline", "xline", None),
        check_vma=False,
    )
```

```python
import jax
import jax.numpy as jnp
import numpy as np
from jax import lax
from jax.experimental import pallas as pl
from jax.experimental.pallas import tpu as pltpu
from jax.sharding import PartitionSpec as P

CLASSES = 8
BI = 2
BX = 2
CH = 32
CAP = 4
ALL = ("inline", "xline")
BF = jnp.bfloat16
F32 = jnp.float32
CELLS = CLASSES * BI * BX


def iota(shape, dim):
    return lax.broadcasted_iota(jnp.int32, shape, dim)


def nt(a, b):
    return lax.dot_general(a, b, (((1,), (1,)), ((), ())), preferred_element_type=F32)


def tn(a, b):
    return lax.dot_general(a, b, (((0,), (0,)), ((), ())), preferred_element_type=F32)


def nn(a, b):
    return jnp.dot(a, b, preferred_element_type=F32)


def before(count):
    return (iota((count, count), 0) < iota((count, count), 1)).astype(BF)


def pack_kernel(
    dest_ref, bin_ref, class_ref, traces_ref, out_ref, tags, loaded, packed, tag_sem, load_sem, store_sem
):
    rows, width = packed.shape
    count, half = loaded.shape[0] // 2, loaded.shape[1]
    devices = rows // (2 * CAP)
    parts = store_sem.shape[0]
    each = rows // parts
    small = []
    for number, ref in enumerate((dest_ref, bin_ref, class_ref)):
        small.append(pltpu.make_async_copy(ref, tags.at[number], tag_sem.at[number]))
        small[-1].start()
    loads = []
    for side in range(2):
        loads.append(
            pltpu.make_async_copy(
                traces_ref.at[:, pl.ds(side * half, half)],
                loaded.at[pl.ds(side * count, count)],
                load_sem.at[side],
            )
        )
        loads[-1].start()
    for copy in small:
        copy.wait()
    dest = tags[0]
    named = iota((devices, count), 0) == dest
    rank = nn(named.astype(BF), before(count))
    slot = jnp.sum(jnp.where(named, rank, 0.0), axis=0, keepdims=True)
    position = dest * (2 * CAP) + slot.astype(jnp.int32)
    cell = tags[1] * CLASSES + tags[2]
    lane = iota((128, count), 0)
    tagged = jnp.concatenate(
        [((lane == cell) | (lane == 127)).astype(BF), (lane == cell + CELLS).astype(BF)], axis=1
    )
    for load in loads:
        load.wait()
    stores = []
    for part in range(parts):
        piece = slice(part * each, (part + 1) * each)
        row = iota((each, count), 0) + part * each
        place = jnp.concatenate(
            [(row == position).astype(BF), (row == position + CAP).astype(BF)], axis=1
        )
        packed[piece, half:] = nt(place, tagged).astype(BF)
        packed[piece, :half] = nn(place, loaded[...]).astype(BF)
        chunk = pl.ds(part * each, each)
        stores.append(pltpu.make_async_copy(packed.at[chunk], out_ref.at[chunk], store_sem.at[part]))
        stores[-1].start()
    for copy in stores:
        copy.wait()


def pack(traces, dest, bins, classes, devices):
    count, samples = traces.shape
    rows, width = devices * 2 * CAP, samples // 2 + 128
    kept = pl.BlockSpec(memory_space=pltpu.HBM)
    pin = lambda array: pltpu.with_memory_space_constraint(array, pltpu.HBM)
    return pl.pallas_call(
        pack_kernel,
        in_specs=[kept] * 4,
        out_specs=kept,
        out_shape=pltpu.HBM((rows, width), BF),
        scratch_shapes=[
            pltpu.VMEM((3, 1, count), jnp.int32),
            pltpu.VMEM((2 * count, samples // 2), BF),
            pltpu.VMEM((rows, width), BF),
            pltpu.SemaphoreType.DMA((3,)),
            pltpu.SemaphoreType.DMA((2,)),
            pltpu.SemaphoreType.DMA((8,)),
        ],
        compiler_params=pltpu.CompilerParams(vmem_limit_bytes=24 << 20),
        name="pack",
    )(pin(dest), pin(bins), pin(classes), pin(traces))


def stack_kernel(arrived_ref, out_ref):
    width = arrived_ref.shape[1]
    half = width - 128
    stacked = tn(arrived_ref[:, half:], arrived_ref[...])
    fold = jnp.maximum(stacked[:CELLS, width - 1 : width], 1.0)
    out_ref[:, :half] = (stacked[:CELLS, :half] / fold).astype(BF)
    out_ref[:, half:] = (stacked[CELLS : 2 * CELLS, :half] / fold).astype(BF)


def stack(arrived):
    rows, width = arrived.shape
    whole = pl.BlockSpec(memory_space=pltpu.VMEM)
    return pl.pallas_call(
        stack_kernel,
        in_specs=[whole],
        out_specs=whole,
        out_shape=jax.ShapeDtypeStruct((CELLS, 2 * (width - 128)), BF),
        compiler_params=pltpu.CompilerParams(vmem_limit_bytes=12 << 20),
        name="stack",
    )(arrived)


def band_loads(source_ref, weights, sem, sizes):
    loads, first = {}, 0
    for number, size in enumerate(sizes):
        blocks = pl.ds(first, size)
        loads[first] = pltpu.make_async_copy(source_ref.at[:, blocks], weights.at[:, blocks], sem.at[number])
        loads[first].start()
        first += size
    return loads


def moved_block(averaged, weights, block, loads):
    if block in loads:
        loads[block].wait()
    classes, _, _, band = weights.shape
    start = block * band
    wide = jnp.concatenate([weights[number, block] for number in range(classes)], axis=1)
    moved = nn(averaged[:, start : start + 2 * band], wide)
    kind = iota((averaged.shape[0], band), 0) % classes
    total = moved[:, :band]
    for number in range(1, classes):
        total = jnp.where(kind == number, moved[:, number * band : (number + 1) * band], total)
    return total.astype(BF)


BAND_SIZES = (2, 2, 2, 2, 2, 2, 2, 2)


def band_kernel(averaged_ref, band_ref, out_ref, weights, padded, sem):
    loads = band_loads(band_ref, weights, sem, BAND_SIZES)
    rows, samples = averaged_ref.shape
    band = weights.shape[3]
    padded[:, :samples] = averaged_ref[...]
    padded[:, samples:] = jnp.zeros((rows, band), BF)
    for block in range(weights.shape[1]):
        out_ref[:, block * band : (block + 1) * band] = moved_block(padded, weights, block, loads)


def moved_out(averaged, weights):
    rows, samples = averaged.shape
    whole = pl.BlockSpec(memory_space=pltpu.VMEM)
    return pl.pallas_call(
        band_kernel,
        in_specs=[whole, pl.BlockSpec(memory_space=pltpu.HBM)],
        out_specs=(whole, whole),
        out_shape=(jax.ShapeDtypeStruct((rows, samples), BF), jax.ShapeDtypeStruct(weights.shape, BF)),
        scratch_shapes=[
            pltpu.VMEM((rows, samples + weights.shape[3]), BF),
            pltpu.SemaphoreType.DMA((len(BAND_SIZES),)),
        ],
        compiler_params=pltpu.CompilerParams(vmem_limit_bytes=16 << 20),
        name="band",
    )(averaged, pltpu.with_memory_space_constraint(weights, pltpu.HBM))


def border_kernel(
    place_ref, one_ref, other_ref, own_ref, weights, column_ref, top_ref, bottom_ref, padded
):
    samples = own_ref.shape[1]
    band = weights.shape[3]
    odd = place_ref[0] % 2 == 1
    one, other = one_ref[...], other_ref[...]
    padded[:CELLS, :samples] = jnp.where(odd, one, other)
    padded[CELLS:, :samples] = jnp.where(odd, other, one)
    padded[:, samples:] = jnp.zeros((2 * CELLS, band), BF)
    own = own_ref[...]
    column_ref[CELLS : 2 * CELLS, :] = own
    top_ref[CELLS:, :] = own[: CELLS // 2]
    bottom_ref[: CELLS // 2, :] = own[CELLS // 2 :]
    for block in range(weights.shape[1]):
        lanes = slice(block * band, (block + 1) * band)
        total = moved_block(padded, weights, block, {})
        column_ref[:CELLS, lanes] = total[:CELLS]
        column_ref[2 * CELLS :, lanes] = total[CELLS:]
        top_ref[:CELLS, lanes] = total[:CELLS]
        bottom_ref[CELLS // 2 :, lanes] = total[CELLS:]


def border(place, one, other, own, weights):
    samples = own.shape[1]
    whole = pl.BlockSpec(memory_space=pltpu.VMEM)
    return pl.pallas_call(
        border_kernel,
        in_specs=[pl.BlockSpec(memory_space=pltpu.SMEM)] + [whole] * 4,
        out_specs=(whole, whole, whole),
        out_shape=(
            jax.ShapeDtypeStruct((3 * CELLS, samples), BF),
            jax.ShapeDtypeStruct((3 * CELLS // 2, samples), BF),
            jax.ShapeDtypeStruct((3 * CELLS // 2, samples), BF),
        ),
        scratch_shapes=[pltpu.VMEM((2 * CELLS, samples + weights.shape[3]), BF)],
        compiler_params=pltpu.CompilerParams(vmem_limit_bytes=16 << 20),
        name="border",
    )(place, one, other, own, weights)


TILE = 2048
PART = 1024
WIDE = BX * CH
EDGE = 128
ALL_LINES = BI + 4
TALL = BX * CLASSES


def taps_of(padded, rows, start, size):
    window = padded[rows, start : start + size + 2 * EDGE]
    inner = slice(EDGE, EDGE + size)
    width = window.shape[1]
    return pltpu.roll(window, 1, 1)[:, inner], window[:, inner], pltpu.roll(window, width - 1, 1)[:, inner]


def clear_edges(padded):
    zeros = jnp.zeros((padded.shape[0], EDGE), BF)
    padded[:, :EDGE] = zeros
    padded[:, padded.shape[1] - EDGE :] = zeros


def inside(place_ref, start_x, line):
    bin_x = iota((WIDE, 1), 0) // CH + start_x + place_ref[1] * BX - 1
    bin_i = line + place_ref[0] * BI - 1
    return (bin_x >= 0) & (bin_x < place_ref[3]) & (bin_i >= 0) & (bin_i < place_ref[2])


def run_tiles(columns, first, second, keeps, split, store, volume, taps, hidden):
    samples = volume.shape[1] - 2 * EDGE
    count = len(columns)
    group = 3 * count * TALL
    clear_edges(volume)
    clear_edges(hidden)
    for which, column in enumerate(columns):
        at = 3 * which * CELLS
        for piece in column:
            volume[at : at + piece.shape[0], EDGE : EDGE + samples] = piece[...]
            at += piece.shape[0]

    def first_convolution(start):
        lanes = slice(start, start + TILE)
        for which in range(count):
            rows = slice(3 * which * CELLS, 3 * (which + 1) * CELLS)
            for tap, value in enumerate(taps_of(volume, rows, start, TILE)):
                for line in range(ALL_LINES):
                    at = line * group + (tap * count + which) * TALL
                    taps[at : at + TALL, lanes] = value[line * TALL : (line + 1) * TALL]
        for line in range(BI + 2):
            rows = slice(line * WIDE, (line + 1) * WIDE)
            value = split(nn(first, taps[line * group : (line + 3) * group, lanes]), rows, lanes)
            value = jnp.where(keeps[line], jax.nn.gelu(value), 0.0).astype(BF)
            hidden[rows, EDGE + start : EDGE + start + TILE] = value

    def second_convolution(start):
        for at in range(start, start + TILE, PART):
            held = jnp.concatenate(taps_of(hidden, slice(None), at, PART), axis=0)
            store(nn(second, held), slice(at, at + PART))

    for start in range(0, samples, TILE):
        first_convolution(start)
        if start:
            second_convolution(start - TILE)
    second_convolution(samples - TILE)


def near_kernel(
    place_ref, mid_ref, top_ref, bottom_ref, first_ref, second_ref,
    partial_ref, sum_ref, volume, taps, hidden,
):
    start_x = jnp.where(place_ref[1] % 2 == 0, BX, 0)
    keeps = [inside(place_ref, start_x, line) for line in range(BI + 2)]

    def split(both, rows, lanes):
        partial_ref[rows, lanes] = both[WIDE:]
        return both[:WIDE]

    def store(value, lanes):
        sum_ref[:, lanes] = value

    run_tiles(
        ((mid_ref,), (top_ref, bottom_ref)), first_ref[...], second_ref[...], keeps, split, store,
        volume, taps, hidden,
    )


def far_kernel(
    place_ref, far_ref, partial_ref, sum_ref, first_ref, second_ref, out_ref, volume, taps, hidden, made, sem,
):
    copies = []
    start_x = jnp.where(place_ref[1] % 2 == 0, 0, BX)
    keeps = [inside(place_ref, start_x, line) for line in range(BI + 2)]

    def split(value, rows, lanes):
        return value + partial_ref[rows, lanes]

    def store(value, lanes):
        total = (value + sum_ref[:, lanes]).astype(BF)
        number = lanes.start // PART
        made[number] = total.reshape(made.shape[1:])
        copies.append(
            pltpu.make_async_copy(made.at[number], out_ref.at[:, :, :, pl.ds(lanes.start, PART)], sem.at[number])
        )
        copies[-1].start()

    run_tiles(
        ((far_ref,),), first_ref[...], second_ref[...], keeps, split, store, volume, taps, hidden,
    )
    for copy in copies:
        copy.wait()


def convolutions(place, mid, top, bottom, far, matrices):
    samples = mid.shape[1]
    first_near, first_far, second_near, second_far = matrices
    whole = pl.BlockSpec(memory_space=pltpu.VMEM)
    scalars = pl.BlockSpec(memory_space=pltpu.SMEM)
    bins = (BI + 2) * WIDE

    def buffers(count):
        return [
            pltpu.VMEM((3 * count * CELLS, samples + 2 * EDGE), BF),
            pltpu.VMEM((3 * count * ALL_LINES * TALL, samples), BF),
            pltpu.VMEM((bins, samples + 2 * EDGE), BF),
        ]

    partial, total = pl.pallas_call(
        near_kernel,
        in_specs=[scalars] + [whole] * 5,
        out_specs=(whole, whole),
        out_shape=(
            jax.ShapeDtypeStruct((bins, samples), F32),
            jax.ShapeDtypeStruct((CH * BI * BX, samples), F32),
        ),
        scratch_shapes=buffers(2),
        compiler_params=pltpu.CompilerParams(vmem_limit_bytes=24 << 20),
        cost_estimate=pl.CostEstimate(flops=0, bytes_accessed=0, transcendentals=0),
        name="near",
    )(place, mid, top, bottom, first_near, second_near)
    return pl.pallas_call(
        far_kernel,
        in_specs=[scalars] + [whole] * 5,
        out_specs=pl.BlockSpec(memory_space=pltpu.HBM),
        out_shape=pltpu.HBM((CH, BI, BX, samples), BF),
        scratch_shapes=buffers(1)
        + [
            pltpu.VMEM((samples // PART, CH, BI, BX, PART), BF),
            pltpu.SemaphoreType.DMA((samples // PART,)),
        ],
        compiler_params=pltpu.CompilerParams(vmem_limit_bytes=24 << 20),
        name="far",
    )(place, far, partial, total, first_far, second_far)


def first_matrices(kernel, odd):
    spatial = kernel.transpose(2, 3, 4, 1, 0)
    placed = [
        jnp.pad(spatial, ((0, 0), (at, BX + 1 - at), (0, 0), (0, 0), (0, 0))) for at in range(BX + 2)
    ]
    matrix = jnp.stack(placed, axis=0).transpose(0, 5, 1, 3, 2, 4)
    mirrored = jnp.concatenate([matrix[BX:], matrix[:BX]], axis=0)
    mirrored = jnp.concatenate(
        [mirrored[..., 2 * BX :, :], mirrored[..., BX : 2 * BX, :], mirrored[..., :BX, :]], axis=4
    )
    matrix = jnp.where(odd, mirrored, matrix)
    near = jnp.concatenate([matrix[BX:, ..., BX:, :], matrix[:BX, ..., BX:, :]], axis=0)
    far = matrix[:BX, ..., :BX, :]
    return near.reshape(2 * WIDE, -1), far.reshape(WIDE, -1)


def second_matrices(kernel, odd):
    spatial = kernel.transpose(2, 3, 4, 0, 1)
    placed = [
        [
            jnp.pad(spatial, ((i, BI - 1 - i), (x, BX - 1 - x), (0, 0), (0, 0), (0, 0)))
            for x in range(BX)
        ]
        for i in range(BI)
    ]
    matrix = jnp.stack([jnp.stack(line, axis=0) for line in placed], axis=0)
    matrix = matrix.transpose(4, 5, 0, 1, 2, 3, 6)
    low, high = matrix[..., :BX, :], matrix[..., BX:, :]
    rows = CH * BI * BX
    near, far = jnp.where(odd, low, high), jnp.where(odd, high, low)
    return tuple(jnp.moveaxis(side, 0, 3).reshape(rows, -1) for side in (near, far))


def swapped(block, axis, start):
    count = lax.axis_size(axis)
    pairs = [(i, i + 1) for i in range(start, count - 1, 2)]
    return lax.ppermute(block, axis, pairs + [(j, i) for i, j in pairs])


def per_device(traces, trace_dest, trace_bin, trace_class, band_weights, conv_first, conv_second):
    inline_size = lax.axis_size("inline")
    xline_size = lax.axis_size("xline")
    devices = inline_size * xline_size
    at_i, at_x = lax.axis_index("inline"), lax.axis_index("xline")
    count, samples = traces.shape
    width = samples // 2 + 128
    outgoing = pack(
        traces,
        trace_dest.reshape(1, count),
        trace_bin.reshape(1, count),
        trace_class.reshape(1, count),
        devices,
    )
    arrived = lax.all_to_all(
        outgoing.reshape(devices, 2 * CAP, width), ALL, split_axis=0, concat_axis=0, tiled=True
    ).reshape(devices * 2 * CAP, width)
    odd_x = at_x % 2 == 1
    place = jnp.stack(
        [at_i, at_x, jnp.int32(inline_size * BI), jnp.int32(xline_size * BX)]
    ).astype(jnp.int32)
    matrices = first_matrices(conv_first, odd_x) + second_matrices(conv_second, odd_x)
    arrived, matrices, place = lax.optimization_barrier((arrived, matrices, place))
    classes, blocks, steps, band, _ = band_weights.shape
    weights = band_weights.reshape(classes, blocks, steps * band, band)
    averaged = stack(arrived)
    one, other = swapped(averaged, "inline", 0), swapped(averaged, "inline", 1)
    volume, weights = moved_out(averaged, weights)
    column, top, bottom = border(place, one, other, volume, weights)
    far = swapped(column, "xline", 1)
    top, bottom = swapped(top, "xline", 0), swapped(bottom, "xline", 0)
    return convolutions(place, column, top, bottom, far, matrices)


def solution(mesh):
    return jax.shard_map(
        per_device,
        mesh=mesh,
        in_specs=(
            P(ALL, None),
            P(ALL, None),
            P(ALL),
            P(ALL),
            P(),
            P(),
            P(),
        ),
        out_specs=P(None, "inline", "xline", None),
        check_vma=False,
    )
```

```python
import jax
import jax.numpy as jnp
import numpy as np
from jax import lax
from jax.experimental import pallas as pl
from jax.experimental.pallas import tpu as pltpu
from jax.sharding import PartitionSpec as P

CLASSES = 8
BI = 2
BX = 2
CH = 32
CAP = 4
ALL = ("inline", "xline")
BF = jnp.bfloat16
F32 = jnp.float32
CELLS = CLASSES * BI * BX


def iota(shape, dim):
    return lax.broadcasted_iota(jnp.int32, shape, dim)


def nt(a, b):
    return lax.dot_general(a, b, (((1,), (1,)), ((), ())), preferred_element_type=F32)


def tn(a, b):
    return lax.dot_general(a, b, (((0,), (0,)), ((), ())), preferred_element_type=F32)


def nn(a, b):
    return jnp.dot(a, b, preferred_element_type=F32)


def before(count):
    return (iota((count, count), 0) < iota((count, count), 1)).astype(BF)


def pack_kernel(
    dest_ref, bin_ref, class_ref, traces_ref, out_ref, tags, loaded, packed, tag_sem, load_sem, store_sem
):
    rows, width = packed.shape
    count, half = loaded.shape[0] // 2, loaded.shape[1]
    devices = rows // (2 * CAP)
    parts = store_sem.shape[0]
    each = rows // parts
    small = []
    for number, ref in enumerate((dest_ref, bin_ref, class_ref)):
        small.append(pltpu.make_async_copy(ref, tags.at[number], tag_sem.at[number]))
        small[-1].start()
    loads = []
    for side in range(2):
        loads.append(
            pltpu.make_async_copy(
                traces_ref.at[:, pl.ds(side * half, half)],
                loaded.at[pl.ds(side * count, count)],
                load_sem.at[side],
            )
        )
        loads[-1].start()
    for copy in small:
        copy.wait()
    dest = tags[0]
    named = iota((devices, count), 0) == dest
    rank = nn(named.astype(BF), before(count))
    slot = jnp.sum(jnp.where(named, rank, 0.0), axis=0, keepdims=True)
    position = dest * (2 * CAP) + slot.astype(jnp.int32)
    cell = tags[1] * CLASSES + tags[2]
    lane = iota((128, count), 0)
    tagged = jnp.concatenate(
        [((lane == cell) | (lane == 127)).astype(BF), (lane == cell + CELLS).astype(BF)], axis=1
    )
    for load in loads:
        load.wait()
    stores = []
    for part in range(parts):
        piece = slice(part * each, (part + 1) * each)
        row = iota((each, count), 0) + part * each
        place = jnp.concatenate(
            [(row == position).astype(BF), (row == position + CAP).astype(BF)], axis=1
        )
        packed[piece, half:] = nt(place, tagged).astype(BF)
        packed[piece, :half] = nn(place, loaded[...]).astype(BF)
        chunk = pl.ds(part * each, each)
        stores.append(pltpu.make_async_copy(packed.at[chunk], out_ref.at[chunk], store_sem.at[part]))
        stores[-1].start()
    for copy in stores:
        copy.wait()


def pack(traces, dest, bins, classes, devices):
    count, samples = traces.shape
    rows, width = devices * 2 * CAP, samples // 2 + 128
    kept = pl.BlockSpec(memory_space=pltpu.HBM)
    pin = lambda array: pltpu.with_memory_space_constraint(array, pltpu.HBM)
    return pl.pallas_call(
        pack_kernel,
        in_specs=[kept] * 4,
        out_specs=kept,
        out_shape=pltpu.HBM((rows, width), BF),
        scratch_shapes=[
            pltpu.VMEM((3, 1, count), jnp.int32),
            pltpu.VMEM((2 * count, samples // 2), BF),
            pltpu.VMEM((rows, width), BF),
            pltpu.SemaphoreType.DMA((3,)),
            pltpu.SemaphoreType.DMA((2,)),
            pltpu.SemaphoreType.DMA((4,)),
        ],
        compiler_params=pltpu.CompilerParams(vmem_limit_bytes=24 << 20),
        name="pack",
    )(pin(dest), pin(bins), pin(classes), pin(traces))


def stack_kernel(arrived_ref, out_ref):
    width = arrived_ref.shape[1]
    half = width - 128
    stacked = tn(arrived_ref[:, half:], arrived_ref[...])
    fold = jnp.maximum(stacked[:CELLS, width - 1 : width], 1.0)
    out_ref[:, :half] = (stacked[:CELLS, :half] / fold).astype(BF)
    out_ref[:, half:] = (stacked[CELLS : 2 * CELLS, :half] / fold).astype(BF)


def stack(arrived):
    rows, width = arrived.shape
    whole = pl.BlockSpec(memory_space=pltpu.VMEM)
    return pl.pallas_call(
        stack_kernel,
        in_specs=[whole],
        out_specs=whole,
        out_shape=jax.ShapeDtypeStruct((CELLS, 2 * (width - 128)), BF),
        compiler_params=pltpu.CompilerParams(vmem_limit_bytes=12 << 20),
        name="stack",
    )(arrived)


def band_loads(source_ref, weights, sem, sizes):
    loads, first = {}, 0
    for number, size in enumerate(sizes):
        blocks = pl.ds(first, size)
        loads[first] = pltpu.make_async_copy(source_ref.at[:, blocks], weights.at[:, blocks], sem.at[number])
        loads[first].start()
        first += size
    return loads


def moved_block(averaged, weights, block, loads):
    if block in loads:
        loads[block].wait()
    classes, _, _, band = weights.shape
    start = block * band
    wide = jnp.concatenate([weights[number, block] for number in range(classes)], axis=1)
    moved = nn(averaged[:, start : start + 2 * band], wide)
    kind = iota((averaged.shape[0], band), 0) % classes
    total = moved[:, :band]
    for number in range(1, classes):
        total = jnp.where(kind == number, moved[:, number * band : (number + 1) * band], total)
    return total.astype(BF)


BAND_SIZES = (3, 3, 3, 3, 2, 1, 1)


def band_kernel(averaged_ref, band_ref, out_ref, weights, padded, sem):
    loads = band_loads(band_ref, weights, sem, BAND_SIZES)
    rows, samples = averaged_ref.shape
    band = weights.shape[3]
    padded[:, :samples] = averaged_ref[...]
    padded[:, samples:] = jnp.zeros((rows, band), BF)
    for block in range(weights.shape[1]):
        out_ref[:, block * band : (block + 1) * band] = moved_block(padded, weights, block, loads)


def moved_out(averaged, weights):
    rows, samples = averaged.shape
    whole = pl.BlockSpec(memory_space=pltpu.VMEM)
    return pl.pallas_call(
        band_kernel,
        in_specs=[whole, pl.BlockSpec(memory_space=pltpu.HBM)],
        out_specs=(whole, whole),
        out_shape=(jax.ShapeDtypeStruct((rows, samples), BF), jax.ShapeDtypeStruct(weights.shape, BF)),
        scratch_shapes=[
            pltpu.VMEM((rows, samples + weights.shape[3]), BF),
            pltpu.SemaphoreType.DMA((len(BAND_SIZES),)),
        ],
        compiler_params=pltpu.CompilerParams(vmem_limit_bytes=16 << 20),
        name="band",
    )(averaged, pltpu.with_memory_space_constraint(weights, pltpu.HBM))


def border_kernel(
    place_ref, one_ref, other_ref, own_ref, weights, column_ref, top_ref, bottom_ref, padded
):
    samples = own_ref.shape[1]
    band = weights.shape[3]
    odd = place_ref[0] % 2 == 1
    one, other = one_ref[...], other_ref[...]
    padded[:CELLS, :samples] = jnp.where(odd, one, other)
    padded[CELLS:, :samples] = jnp.where(odd, other, one)
    padded[:, samples:] = jnp.zeros((2 * CELLS, band), BF)
    own = own_ref[...]
    column_ref[CELLS : 2 * CELLS, :] = own
    top_ref[CELLS:, :] = own[: CELLS // 2]
    bottom_ref[: CELLS // 2, :] = own[CELLS // 2 :]
    for block in range(weights.shape[1]):
        lanes = slice(block * band, (block + 1) * band)
        total = moved_block(padded, weights, block, {})
        column_ref[:CELLS, lanes] = total[:CELLS]
        column_ref[2 * CELLS :, lanes] = total[CELLS:]
        top_ref[:CELLS, lanes] = total[:CELLS]
        bottom_ref[CELLS // 2 :, lanes] = total[CELLS:]


def border(place, one, other, own, weights):
    samples = own.shape[1]
    whole = pl.BlockSpec(memory_space=pltpu.VMEM)
    return pl.pallas_call(
        border_kernel,
        in_specs=[pl.BlockSpec(memory_space=pltpu.SMEM)] + [whole] * 4,
        out_specs=(whole, whole, whole),
        out_shape=(
            jax.ShapeDtypeStruct((3 * CELLS, samples), BF),
            jax.ShapeDtypeStruct((3 * CELLS // 2, samples), BF),
            jax.ShapeDtypeStruct((3 * CELLS // 2, samples), BF),
        ),
        scratch_shapes=[pltpu.VMEM((2 * CELLS, samples + weights.shape[3]), BF)],
        compiler_params=pltpu.CompilerParams(vmem_limit_bytes=16 << 20),
        name="border",
    )(place, one, other, own, weights)


TILE = 2048
WIDE = BX * CH
EDGE = 128
ALL_LINES = BI + 4
TALL = BX * CLASSES


def taps_of(padded, rows, start):
    window = padded[rows, start : start + TILE + 2 * EDGE]
    inner = slice(EDGE, EDGE + TILE)
    width = window.shape[1]
    return pltpu.roll(window, 1, 1)[:, inner], window[:, inner], pltpu.roll(window, width - 1, 1)[:, inner]


def clear_edges(padded):
    zeros = jnp.zeros((padded.shape[0], EDGE), BF)
    padded[:, :EDGE] = zeros
    padded[:, padded.shape[1] - EDGE :] = zeros


def inside(place_ref, start_x, line):
    bin_x = iota((WIDE, 1), 0) // CH + start_x + place_ref[1] * BX - 1
    bin_i = line + place_ref[0] * BI - 1
    return (bin_x >= 0) & (bin_x < place_ref[3]) & (bin_i >= 0) & (bin_i < place_ref[2])


def run_tiles(columns, first, second, keeps, split, store, volume, taps, hidden):
    samples = volume.shape[1] - 2 * EDGE
    count = len(columns)
    group = 3 * count * TALL
    clear_edges(volume)
    clear_edges(hidden)
    for which, column in enumerate(columns):
        at = 3 * which * CELLS
        for piece in column:
            volume[at : at + piece.shape[0], EDGE : EDGE + samples] = piece[...]
            at += piece.shape[0]

    def first_convolution(start):
        lanes = slice(start, start + TILE)
        for which in range(count):
            rows = slice(3 * which * CELLS, 3 * (which + 1) * CELLS)
            for tap, value in enumerate(taps_of(volume, rows, start)):
                for line in range(ALL_LINES):
                    at = line * group + (tap * count + which) * TALL
                    taps[at : at + TALL, lanes] = value[line * TALL : (line + 1) * TALL]
        for line in range(BI + 2):
            rows = slice(line * WIDE, (line + 1) * WIDE)
            value = split(nn(first, taps[line * group : (line + 3) * group, lanes]), rows, lanes)
            value = jnp.where(keeps[line], jax.nn.gelu(value), 0.0).astype(BF)
            hidden[rows, EDGE + start : EDGE + start + TILE] = value

    def second_convolution(start):
        held = jnp.concatenate(taps_of(hidden, slice(None), start), axis=0)
        store(nn(second, held), slice(start, start + TILE))

    for start in range(0, samples, TILE):
        first_convolution(start)
        if start:
            second_convolution(start - TILE)
    second_convolution(samples - TILE)


def near_kernel(
    place_ref, mid_ref, top_ref, bottom_ref, first_ref, second_ref,
    partial_ref, sum_ref, volume, taps, hidden,
):
    start_x = jnp.where(place_ref[1] % 2 == 0, BX, 0)
    keeps = [inside(place_ref, start_x, line) for line in range(BI + 2)]

    def split(both, rows, lanes):
        partial_ref[rows, lanes] = both[WIDE:]
        return both[:WIDE]

    def store(value, lanes):
        sum_ref[:, lanes] = value

    run_tiles(
        ((mid_ref,), (top_ref, bottom_ref)), first_ref[...], second_ref[...], keeps, split, store,
        volume, taps, hidden,
    )


def far_kernel(
    place_ref, far_ref, partial_ref, sum_ref, first_ref, second_ref, out_ref, volume, taps, hidden,
):
    start_x = jnp.where(place_ref[1] % 2 == 0, 0, BX)
    keeps = [inside(place_ref, start_x, line) for line in range(BI + 2)]

    def split(value, rows, lanes):
        return value + partial_ref[rows, lanes]

    def store(value, lanes):
        total = (value + sum_ref[:, lanes]).astype(BF)
        out_ref[:, :, :, lanes] = total.reshape(out_ref.shape[:3] + (TILE,))

    run_tiles(
        ((far_ref,),), first_ref[...], second_ref[...], keeps, split, store, volume, taps, hidden,
    )


def convolutions(place, mid, top, bottom, far, matrices):
    samples = mid.shape[1]
    first_near, first_far, second_near, second_far = matrices
    whole = pl.BlockSpec(memory_space=pltpu.VMEM)
    scalars = pl.BlockSpec(memory_space=pltpu.SMEM)
    bins = (BI + 2) * WIDE

    def buffers(count):
        return [
            pltpu.VMEM((3 * count * CELLS, samples + 2 * EDGE), BF),
            pltpu.VMEM((3 * count * ALL_LINES * TALL, samples), BF),
            pltpu.VMEM((bins, samples + 2 * EDGE), BF),
        ]

    partial, total = pl.pallas_call(
        near_kernel,
        in_specs=[scalars] + [whole] * 5,
        out_specs=(whole, whole),
        out_shape=(
            jax.ShapeDtypeStruct((bins, samples), F32),
            jax.ShapeDtypeStruct((CH * BI * BX, samples), F32),
        ),
        scratch_shapes=buffers(2),
        compiler_params=pltpu.CompilerParams(vmem_limit_bytes=24 << 20),
        cost_estimate=pl.CostEstimate(flops=0, bytes_accessed=0, transcendentals=0),
        name="near",
    )(place, mid, top, bottom, first_near, second_near)
    return pl.pallas_call(
        far_kernel,
        in_specs=[scalars] + [whole] * 5,
        out_specs=whole,
        out_shape=jax.ShapeDtypeStruct((CH, BI, BX, samples), BF),
        scratch_shapes=buffers(1),
        compiler_params=pltpu.CompilerParams(vmem_limit_bytes=24 << 20),
        name="far",
    )(place, far, partial, total, first_far, second_far)


def first_matrices(kernel, odd):
    spatial = kernel.transpose(2, 3, 4, 1, 0)
    placed = [
        jnp.pad(spatial, ((0, 0), (at, BX + 1 - at), (0, 0), (0, 0), (0, 0))) for at in range(BX + 2)
    ]
    matrix = jnp.stack(placed, axis=0).transpose(0, 5, 1, 3, 2, 4)
    mirrored = jnp.concatenate([matrix[BX:], matrix[:BX]], axis=0)
    mirrored = jnp.concatenate(
        [mirrored[..., 2 * BX :, :], mirrored[..., BX : 2 * BX, :], mirrored[..., :BX, :]], axis=4
    )
    matrix = jnp.where(odd, mirrored, matrix)
    near = jnp.concatenate([matrix[BX:, ..., BX:, :], matrix[:BX, ..., BX:, :]], axis=0)
    far = matrix[:BX, ..., :BX, :]
    return near.reshape(2 * WIDE, -1), far.reshape(WIDE, -1)


def second_matrices(kernel, odd):
    spatial = kernel.transpose(2, 3, 4, 0, 1)
    placed = [
        [
            jnp.pad(spatial, ((i, BI - 1 - i), (x, BX - 1 - x), (0, 0), (0, 0), (0, 0)))
            for x in range(BX)
        ]
        for i in range(BI)
    ]
    matrix = jnp.stack([jnp.stack(line, axis=0) for line in placed], axis=0)
    matrix = matrix.transpose(4, 5, 0, 1, 2, 3, 6)
    low, high = matrix[..., :BX, :], matrix[..., BX:, :]
    rows = CH * BI * BX
    near, far = jnp.where(odd, low, high), jnp.where(odd, high, low)
    return tuple(jnp.moveaxis(side, 0, 3).reshape(rows, -1) for side in (near, far))


def swapped(block, axis, start):
    count = lax.axis_size(axis)
    pairs = [(i, i + 1) for i in range(start, count - 1, 2)]
    return lax.ppermute(block, axis, pairs + [(j, i) for i, j in pairs])


def per_device(traces, trace_dest, trace_bin, trace_class, band_weights, conv_first, conv_second):
    inline_size = lax.axis_size("inline")
    xline_size = lax.axis_size("xline")
    devices = inline_size * xline_size
    at_i, at_x = lax.axis_index("inline"), lax.axis_index("xline")
    count, samples = traces.shape
    width = samples // 2 + 128
    outgoing = pack(
        traces,
        trace_dest.reshape(1, count),
        trace_bin.reshape(1, count),
        trace_class.reshape(1, count),
        devices,
    )
    arrived = lax.all_to_all(
        outgoing.reshape(devices, 2 * CAP, width), ALL, split_axis=0, concat_axis=0, tiled=True
    ).reshape(devices * 2 * CAP, width)
    odd_x = at_x % 2 == 1
    place = jnp.stack(
        [at_i, at_x, jnp.int32(inline_size * BI), jnp.int32(xline_size * BX)]
    ).astype(jnp.int32)
    matrices = first_matrices(conv_first, odd_x) + second_matrices(conv_second, odd_x)
    arrived, matrices, place = lax.optimization_barrier((arrived, matrices, place))
    classes, blocks, steps, band, _ = band_weights.shape
    weights = band_weights.reshape(classes, blocks, steps * band, band)
    averaged = stack(arrived)
    one, other = swapped(averaged, "inline", 0), swapped(averaged, "inline", 1)
    volume, weights = moved_out(averaged, weights)
    column, top, bottom = border(place, one, other, volume, weights)
    far = swapped(column, "xline", 1)
    top, bottom = swapped(top, "xline", 0), swapped(bottom, "xline", 0)
    return convolutions(place, column, top, bottom, far, matrices)


def solution(mesh):
    return jax.shard_map(
        per_device,
        mesh=mesh,
        in_specs=(
            P(ALL, None),
            P(ALL, None),
            P(ALL),
            P(ALL),
            P(),
            P(),
            P(),
        ),
        out_specs=P(None, "inline", "xline", None),
        check_vma=False,
    )
```
